128 devices in a mesh: row: 8 (over y_hi, x), col: 16 (over y_lo, z, core).
Axes of the slice: x: 4, y: 4 (y_hi: 2, y_lo: 2; y = y_hi * 2 + y_lo), z: 4, core: 2. Of those that a mesh axis runs over, the one named last changes fastest.
Arguments:
- child_pivot: bfloat16 [2, 2048, 2048], P(None, ('row', 'col')), as said below
- child_panel: bfloat16 [8, 16, 128, 2048], P('row', 'col'), may hold values from -1.796875 to 1.796875
- child_map: int32 [2, 64], replicated, may hold values from 0 to 127, as said below
- panel_mask: int32 [2, 64, 16], replicated, may hold values 0 or 1
- parent_front: bfloat16 [16, 8, 128, 8, 16, 128], P(None, 'row', None, None, 'col'), may hold values from -6 to 6
Outputs:
- parent_out: float32 [16, 8, 128, 8, 16, 128], P(None, 'row', None, None, 'col')
The draws below stay inside these ranges and needn't reach their ends.
Inputs may be any that keep to these rules, and one draw needn't show every extreme that they name: `child_pivot`: each child's matrix is symmetric positive definite. `child_map`: within one child the entries are distinct; update block u of a child maps to a parent block congruent to u // 8 modulo 8.
All inputs are finite; a program needn't handle non-finite values.
Results may differ from the reference program's by a relative error of at most 0.0018.
Values may be sent and summed in bfloat16 or wider, within the bound.
No kernel may reach another device: no remote copies, remote signals or barrier semaphores. Data moves between devices by JAX's collectives and lax.ppermute only.
A program may use at most 192 MiB of HBM per device.

```python
import jax
import jax.numpy as jnp
from jax import lax

BLK = 128
PIV = 2048
HALF = 8
UB = 64
PKB = 16
NPB = 128
NP = 16384
RQ = 16
CQ = 8
N_ROW = 8
N_COL = 16


def draw_child_pivot(key, part):
    key = jax.random.fold_in(key, 11)
    noise_key, diag_key = jax.random.split(key)
    noise = jnp.clip(jax.random.normal(noise_key, (2, PIV, PIV), jnp.float32), -3.0, 3.0)
    diagonal = jax.random.uniform(diag_key, (2, PIV), jnp.float32, 3.0, 6.0)
    symmetric = (noise + jnp.swapaxes(noise, 1, 2)) * 0.5 ** 0.5 / PIV ** 0.5
    identity = jnp.eye(PIV, dtype=jnp.float32)
    return (symmetric * (1.0 - identity) + diagonal[:, :, None] * identity).astype(jnp.bfloat16)


def draw_child_map(key, part):
    key = jax.random.fold_in(key, 23)
    keys_all = jax.random.split(key, 2 * N_ROW)

    def one_order(single_key):
        return jax.random.permutation(single_key, 2 * HALF)
    orders = jax.vmap(one_order)(keys_all)[:, :HALF].astype(jnp.int32)
    shifts = jnp.repeat(jnp.array([1, 0], jnp.int32), N_ROW)
    picked = (orders - orders[:, :1] - shifts[:, None]) % (2 * HALF)
    residue = jnp.tile(jnp.arange(N_ROW, dtype=jnp.int32), 2)
    block_ids = picked * N_ROW + residue[:, None]
    return block_ids.reshape(2, N_ROW * HALF).astype(jnp.int32)


def touch_ends(drawn, stream_key, low, top_value):
    dims = drawn.shape
    index_at = [jax.random.randint(jax.random.fold_in(stream_key, axis), (), 0, dims[axis]) for axis in range(len(dims))]
    drawn = drawn.at[tuple(index_at)].set(low)
    longest = dims.index(max(dims))
    index_at[longest] = (index_at[longest] + 1) % dims[longest]
    return drawn.at[tuple(index_at)].set(top_value)


def level_of(key, dims, pieces, least, high):
    gain = 1.0
    for axis_at, blocks in pieces:
        heights = jax.random.uniform(jax.random.fold_in(jax.random.fold_in(key, 6), axis_at), (blocks,), jnp.float32, least / len(pieces), high / len(pieces))
        gain = gain * jnp.repeat(jnp.exp(heights), dims[axis_at] // blocks).reshape((-1,) + (1,) * (len(dims) - 1 - axis_at))
    return gain


def centred(stream_key, extent, scale, bound, pieces=(), held_as=jnp.bfloat16):
    values = scale * jax.random.normal(stream_key, extent, jnp.float32)
    if pieces:
        values = values * level_of(stream_key, extent, pieces, -0.22, 0.18)
    return jnp.clip(values, -bound, bound).astype(held_as)


def setup_inputs(seed: int = 0) -> dict:
    keys = jax.random.split(jax.random.key(seed), 6)
    return {
        "child_pivot": draw_child_pivot(jax.random.fold_in(keys[5], 71), 0),
        "child_panel": centred(keys[1], (N_ROW, N_COL, BLK, PIV), 0.3, 1.796875, ((0, 8), (1, 16))),
        "child_map": draw_child_map(jax.random.fold_in(keys[5], 71), 0),
        "panel_mask": touch_ends((jax.random.randint(keys[3], (2, UB, PKB), 0, 4) < 3).astype(jnp.int32), jax.random.fold_in(keys[3], 1), 0, 1),
        "parent_front": centred(keys[4], (RQ, N_ROW, BLK, CQ, N_COL, BLK), 1.0, 6.0, ((1, 8), (4, 16))),
    }


def reference(child_pivot, child_panel, child_map, panel_mask, parent_front):
    panels = child_panel.reshape(N_ROW, 2, HALF, BLK, PIV).transpose(1, 0, 2, 3, 4).reshape(2, UB, BLK, PIV)
    stacked = jnp.zeros((NPB, BLK, 2 * PIV), jnp.float32)
    for member in range(2):
        factor = jnp.linalg.cholesky(child_pivot[member].astype(jnp.float32))
        keep_cols = jnp.repeat(panel_mask[member].astype(jnp.float32), BLK, axis=1)
        kept_rows = (panels[member].astype(jnp.float32) * keep_cols[:, None, :]).reshape(UB * BLK, PIV)
        solved = jax.scipy.linalg.solve_triangular(factor, kept_rows.T, lower=True).T
        rounded = lax.optimization_barrier(solved.astype(jnp.bfloat16))
        lower_part = rounded.astype(jnp.float32).reshape(UB, BLK, PIV)
        stacked = stacked.at[child_map[member], :, member * PIV:(member + 1) * PIV].set(lower_part)
    flat = stacked.reshape(NP, 2 * PIV)
    front = parent_front.astype(jnp.float32).reshape(NP, NP)
    update = jnp.dot(flat.astype(jnp.float32), flat.T.astype(jnp.float32), precision=lax.Precision.HIGHEST, preferred_element_type=jnp.float32)
    return (front - update).reshape(RQ, N_ROW, BLK, CQ, N_COL, BLK)
```

```python
import functools

import jax
import jax.numpy as jnp
import numpy as np
from jax import lax
from jax.experimental import pallas as pl
from jax.experimental.pallas import tpu as pltpu
from jax.sharding import Mesh, PartitionSpec as P

F32 = jnp.float32
BF16 = jnp.bfloat16
B = 128
PW = 512
VMEM_BYTES = 56 << 20
STRIP = 32
AXES = ("yhi", "x", "ylo", "z", "core")
SIZES = (2, 4, 2, 4, 2)


def split(x):
    hi = x.astype(BF16)
    return hi, (x - hi.astype(F32)).astype(BF16)


def dot_t(x, y):
    return lax.dot_general(x, y, (((1,), (1,)), ((), ())), preferred_element_type=F32)


def dot3_t(xh, xl, yh, yl):
    return dot_t(jnp.concatenate([xh, xh, xl], axis=1), jnp.concatenate([yh, yl, yh], axis=1))


def leaf_inverse(block):
    lane = lax.broadcasted_iota(jnp.int32, (8, B), 1)
    sub = lax.broadcasted_iota(jnp.int32, (8, B), 0)
    rest = [block[8 * i : 8 * i + 8, :] for i in range(B // 8)]
    done = []
    for t in range(B // 8):
        lo = 8 * t
        cols = [[jnp.broadcast_to(x[:, lo + j : lo + j + 1], (8, B)) for x in rest] for j in range(8)]
        rel = lane - lo
        inside = (rel >= 0) & (rel < 8)
        rows = [jnp.where(inside, jnp.where(rel == sub, 1.0, 0.0), rest[0])]
        rows += [jnp.where(inside, 0.0, x) for x in rest[1:]]
        pivots = jnp.ones((8, B), F32)
        for j in range(8):
            pivot = jnp.broadcast_to(cols[j][0][j : j + 1, :], (8, B))
            pivots = jnp.where(sub == j, pivot, pivots)
            recip = 1.0 / pivot
            mult = [x * recip for x in cols[j]]
            mult[0] = jnp.where(sub > j, mult[0], 0.0)
            for jj in range(j + 1, 8):
                head = jnp.broadcast_to(cols[jj][0][j : j + 1, :], (8, B))
                cols[jj] = [x - m * head for x, m in zip(cols[jj], mult)]
            row = jnp.broadcast_to(rows[0][j : j + 1, :], (8, B))
            rows = [x - m * row for x, m in zip(rows, mult)]
        done.append(jnp.where(lane <= sub + lo, rows[0] * lax.rsqrt(pivots), 0.0))
        rest = rows[1:]
    return jnp.concatenate(done, axis=0)


def place_strips(s, at_ref, pieces, work):
    yhi, x, ylo, z, core = (at_ref[i] for i in range(5))
    y = yhi * 2 + ylo
    for ref, far, first in pieces:

        def strip(g, carry, ref=ref, far=far, first=first):
            mid, near = g // 4 + first, g % 4
            xx = (x - jnp.where(core == 0, mid, far)) & 3
            yy = (y - jnp.where(core == 0, far, mid)) & 3
            zz = (z - near) & 3
            row = ((yy // 2) * 4 + xx) * 8 + (yy % 2) * 4 + zz
            rows = pl.ds(pl.multiple_of(g * STRIP, STRIP), STRIP)
            to = pl.ds(pl.multiple_of(row * STRIP, STRIP), STRIP)
            work[to, :] = ref[rows, :].astype(F32)
            return carry

        lax.fori_loop(0, ref.shape[0] // STRIP, strip, 0)


def panel_kernel(s, at_ref, p0, p1, p2a, p2b, p3, *refs):
    prev = [(refs[2 * p], refs[2 * p + 1]) for p in range(s)]
    hi_ref, lo_ref, work = refs[2 * s :]
    n = work.shape[0]
    place_strips(s, at_ref, ((p0, 0, 0), (p1, 1, 0), (p2a, 2, 0), (p2b, 2, 2), (p3, 3, 0)), work)
    nk = PW // B
    base = s * PW

    def load(pair, rows):
        return pair[0][rows, :], pair[1][rows, :]

    right = [load(pair, pl.ds(base, PW)) for pair in prev]
    for rb in range(n // PW):
        first = 0 if rb >= s else rb

        def chunk(c, carry, rb=rb, first=first):
            rows = pl.ds(pl.multiple_of(rb * PW + c * 256, 256), 256)
            total = work[rows, :] if rb >= s else jnp.zeros((256, PW), F32)
            for p in range(first, s):
                total = total - dot3_t(*load(prev[p], rows), *right[p])
            work[rows, :] = total
            return carry

        if s:
            lax.fori_loop(0, PW // 256, chunk, 0)

    eye = (lax.broadcasted_iota(jnp.int32, (B, B), 0) == lax.broadcasted_iota(jnp.int32, (B, B), 1)).astype(F32)

    def step(k, carry):
        cols = pl.ds(pl.multiple_of(k * B, B), B)
        diag = pl.ds(pl.multiple_of(base + k * B, B), B)
        inv = leaf_inverse(work[diag, cols])
        work[diag, cols] = eye
        ih, il = split(inv)

        def scale(c, inner):
            rows = pl.ds(pl.multiple_of(c * 512, 512), 512)
            qh, ql = split(dot3_t(*split(work[rows, cols]), ih, il))
            hi_ref[rows, cols] = qh
            lo_ref[rows, cols] = ql
            return inner

        lax.fori_loop(0, n // 512, scale, 0)
        for kk in range(nk - 1):

            @pl.when(k == kk)
            def _(kk=kk):
                width = (nk - 1 - kk) * B
                at = pl.ds(kk * B, B)
                later = pl.ds((kk + 1) * B, width)
                below = pl.ds(base + (kk + 1) * B, width)
                work[pl.ds(base + kk * B, B), later] = jnp.zeros((B, width), F32)
                yh, yl = hi_ref[below, at], lo_ref[below, at]

                def update(c, inner):
                    rows = pl.ds(pl.multiple_of(c * 512, 512), 512)
                    work[rows, later] = work[rows, later] - dot3_t(hi_ref[rows, at], lo_ref[rows, at], yh, yl)
                    return inner

                lax.fori_loop(0, n // 512, update, 0)
                hi_ref[below, at] = jnp.zeros((width, B), BF16)
                lo_ref[below, at] = jnp.zeros((width, B), BF16)

        return carry

    lax.fori_loop(0, nk, step, 0)


def factor_panel(s, n, at, pieces, prev):
    flat = [x for pair in prev for x in pair]
    full = pl.BlockSpec(memory_space=pltpu.VMEM)
    out = jax.ShapeDtypeStruct((n, PW), BF16)
    return pl.pallas_call(
        functools.partial(panel_kernel, s),
        out_shape=(out, out),
        in_specs=[pl.BlockSpec(memory_space=pltpu.SMEM)] + [full] * (len(pieces) + len(flat)),
        out_specs=(full, full),
        scratch_shapes=[pltpu.VMEM((n, PW), F32)],
        compiler_params=pltpu.CompilerParams(vmem_limit_bytes=VMEM_BYTES),
        cost_estimate=pl.CostEstimate(flops=30 * 10**9, bytes_accessed=10**7, transcendentals=0),
        name="factor_panel",
    )(at, *pieces, *flat)


def times_inverse(x, v_refs, store):
    for s in range(len(v_refs) // 2):
        vh, vl = v_refs[2 * s], v_refs[2 * s + 1]
        part = x[:, : (s + 1) * PW]
        both = jnp.concatenate([part, part], axis=1)
        v = jnp.concatenate([vh[...], vl[...]], axis=0)
        store(s, jnp.dot(both, v, preferred_element_type=F32).astype(BF16))


def v_specs(count):
    specs = []
    for s in range(count):
        spec = pl.BlockSpec(((s + 1) * PW, PW), lambda *_: (0, 0), pipeline_mode=pl.Buffered(1))
        specs += [spec, spec]
    return specs


def solve_rows_kernel(x_ref, *refs):
    out_ref = refs[-1]

    def store(s, value):
        out_ref[:, s * PW : (s + 1) * PW] = value

    times_inverse(x_ref[...], refs[:-1], store)


def solve_rows(x, panels):
    rows, n = x.shape
    tile = 512
    flat = [v for pair in panels for v in pair]
    return pl.pallas_call(
        solve_rows_kernel,
        grid=(rows // tile,),
        out_shape=jax.ShapeDtypeStruct((rows, n), BF16),
        in_specs=[pl.BlockSpec((tile, n), lambda g: (g, 0))] + v_specs(len(panels)),
        out_specs=pl.BlockSpec((tile, n), lambda g: (g, 0)),
        compiler_params=pltpu.CompilerParams(vmem_limit_bytes=VMEM_BYTES),
        name="solve_rows",
    )(x, *flat)


def solve_cols_kernel(count_ref, order_ref, x0_ref, x1_ref, *refs):
    out_ref = refs[-1]

    @pl.when(2 * pl.program_id(1) < count_ref[pl.program_id(0)])
    def _():
        def store(s, value):
            out_ref[0, :, s * PW : (s + 1) * PW] = value

        times_inverse(jnp.concatenate([x0_ref[0], x1_ref[0]], axis=0), refs[:-1], store)


def solve_cols(x, counts, order, panels):
    n = x.shape[2]
    flat = [v for pair in panels for v in pair]
    return pl.pallas_call(
        solve_cols_kernel,
        grid_spec=pltpu.PrefetchScalarGridSpec(
            num_scalar_prefetch=2,
            grid=(2, 4),
            in_specs=[
                pl.BlockSpec((1, B, n), lambda e, g, c, o: (o[e, 2 * g], 0, 0)),
                pl.BlockSpec((1, B, n), lambda e, g, c, o: (o[e, 2 * g + 1], 0, 0)),
            ]
            + v_specs(len(panels)),
            out_specs=pl.BlockSpec((1, 2 * B, n), lambda e, g, c, o: (e, g, 0)),
        ),
        out_shape=jax.ShapeDtypeStruct((2, 8 * B, n), BF16),
        compiler_params=pltpu.CompilerParams(vmem_limit_bytes=VMEM_BYTES),
        name="solve_cols",
    )(counts, order, x, x, *flat)


def extend_kernel(at_ref, count_ref, col_ref, row_ref, front_ref, r0_ref, r1_ref, c0_ref, c1_ref, out_ref, prod):
    total = front_ref.shape[0]
    ylo, z = at_ref[2], at_ref[3]

    def fill(c, carry):
        rows = pl.ds(pl.multiple_of(c * 1024, 1024), 1024)
        out_ref[rows, :] = front_ref[rows, :].astype(F32)
        return carry

    lax.fori_loop(0, total // 1024, fill, 0)
    for a, (r_ref, c_ref) in enumerate(((r0_ref, c0_ref), (r1_ref, c1_ref))):
        count = count_ref[a]

        def pair(g, carry, a=a, r_ref=r_ref, c_ref=c_ref, count=count):
            right = c_ref[pl.ds(pl.multiple_of(g * 2 * B, 2 * B), 2 * B), :]

            def half(h, inner):
                rows = pl.ds(pl.multiple_of(h * 512, 512), 512)
                prod[rows, :] = dot_t(r_ref[rows, :], right)
                return inner

            lax.fori_loop(0, 2, half, 0)
            for m in range(2):

                @pl.when(2 * g + m < count)
                def _(m=m):
                    slot = col_ref[a, 2 * g + m]
                    for b in range(8):
                        block = ((ylo + b) & 1) * 4 + ((z - b // 2) & 3)
                        at = pl.ds(row_ref[a, block] * (8 * B) + slot, B, stride=8)
                        out_ref[at, :] = out_ref[at, :] - prod[b * B : (b + 1) * B, m * B : (m + 1) * B]

            return carry

        lax.fori_loop(0, (count + 1) // 2, pair, 0)


def extend(at, counts, col_slots, row_slots, front, r0, r1, c0, c1):
    smem = pl.BlockSpec(memory_space=pltpu.SMEM)
    vmem = pl.BlockSpec(memory_space=pltpu.VMEM)
    return pl.pallas_call(
        extend_kernel,
        out_shape=jax.ShapeDtypeStruct(front.shape, F32),
        in_specs=[smem] * 4 + [vmem] * 5,
        out_specs=vmem,
        scratch_shapes=[pltpu.VMEM((8 * B, 2 * B), F32)],
        compiler_params=pltpu.CompilerParams(vmem_limit_bytes=VMEM_BYTES),
        name="extend_add",
    )(at, counts, col_slots, row_slots, front, r0, r1, c0, c1)


def move(x, target):
    def flat(c):
        return int(np.ravel_multi_index(c, SIZES))

    pairs = [(flat(c), flat(target(*c))) for c in np.ndindex(*SIZES)]
    return lax.ppermute(x, AXES, pairs)


def step_z(by):
    return lambda yhi, x, ylo, z, core: (yhi, x, ylo, (z + by) % 4, core)


def step_x(by):
    return lambda yhi, x, ylo, z, core: (yhi, (x + by) % 4, ylo, z, core)


def step_y(by):
    def target(yhi, x, ylo, z, core):
        y = (yhi * 2 + ylo + by) % 4
        return (y // 2, x, y % 2, z, core)

    return target


def step_first(by):
    return lambda *c: (step_x(by) if c[4] == 0 else step_y(by))(*c)


def step_second(by):
    return lambda *c: (step_y(by) if c[4] == 0 else step_x(by))(*c)


def ring(x, step):
    half = x.shape[0] // 2
    back = move(x, step(1))
    ahead = move(x, step(-1))
    return x, back, move(back[:half], step(1)), move(ahead[half:], step(-1)), ahead


def join(parts, axis):
    x, back, far0, far1, ahead = parts
    return jnp.stack([x, back, jnp.concatenate([far0, far1], axis=0), ahead], axis=axis)


def swap(x):
    return move(x, lambda yhi, x, ylo, z, core: (yhi, x, ylo, z, 1 - core))


def to_row_group(yhi, x, ylo, z, core):
    i = z * 2 + core
    return (yhi, x, i // 4, i % 4, ylo)


def to_col_group(yhi, x, ylo, z, core):
    r, i = yhi * 4 + x, z * 2 + core
    return (i // 4, i % 4, r % 2, r // 2, ylo)


def pick(x, index):
    return lax.dynamic_index_in_dim(x, index, 0, keepdims=False)


def per_device(child_pivot, child_panel, child_map, panel_mask, parent_front):
    yhi, x, ylo, z, core = (lax.axis_index(name) for name in AXES)
    row = yhi * 4 + x
    y = yhi * 2 + ylo
    at = jnp.stack([yhi, x, ylo, z, core]).astype(jnp.int32)
    n = child_pivot.shape[2]
    np_ = n // PW

    other = swap(pick(child_pivot, 1 - core))
    own = pick(child_pivot, core)
    strip = jnp.where(core == 0, jnp.concatenate([own, other]), jnp.concatenate([other, own]))
    strip = strip.reshape(STRIP, np_, PW).transpose(1, 0, 2)
    near = join(ring(strip, step_z), 1)
    plane = join(ring(near, step_first), 1).reshape(np_, 16 * STRIP, PW)
    pieces = [ring(plane[s], step_second) for s in range(np_)]

    mask = pick(pick(panel_mask, ylo), row * 8 + z * 2 + core)
    kept = (child_panel.reshape(B, n // B, B) * mask.astype(BF16)[None, :, None]).reshape(B, n)
    kept, ready = lax.optimization_barrier((kept, pieces[0][1]))
    pieces[0] = (pieces[0][0], ready) + tuple(pieces[0][2:])
    mine = move(kept, to_col_group)
    col_panel = join(ring(join(ring(mine, step_first), 0), step_second), 0).reshape(16, B, n)
    mine = move(kept, to_row_group)
    pair = jnp.stack([mine, move(mine, lambda yhi, x, ylo, z, core: (yhi, x, 1 - ylo, z, core))])
    row_panel = join(ring(pair, step_z), 0).reshape(8 * B, n)

    maps = child_map.reshape(2, 8, 8)
    maps = jnp.stack([pick(maps, core), pick(maps, 1 - core)])
    slots = maps // 8
    row_slots = lax.dynamic_index_in_dim(slots, row, 1, keepdims=False)
    by_col = lax.dynamic_slice_in_dim(slots, 2 * z, 2, axis=1)
    needed = by_col % 2 == ylo
    place = jnp.cumsum(needed.astype(jnp.int32), axis=2) - 1
    hit = (place[..., None, :] == jnp.arange(8)[:, None]) & needed[..., None, :]
    i = jnp.arange(8)
    dx = (x - i % 4)[None, :] % 4
    dy = (y - (i // 4)[None, :] * 2 - jnp.arange(2)[:, None]) % 4
    dx = jnp.broadcast_to(dx, dy.shape)
    where = jnp.where(core == 0, dy * 4 + dx, dx * 4 + dy)
    order = jnp.sum(jnp.where(hit[0], where[:, None, :], 0), axis=2).astype(jnp.int32)
    col_slots = jnp.sum(jnp.where(hit, (by_col // 2)[..., None, :], 0), axis=3).astype(jnp.int32)
    counts = jnp.sum(needed, axis=2).astype(jnp.int32)

    panels = []
    for s in range(np_):
        panels.append(factor_panel(s, n, at, pieces[s], panels))
    row_side = solve_rows(row_panel, panels)
    row_other = swap(row_side)
    col_side = solve_cols(col_panel, counts[0], order, panels)
    col_other = swap(pick(col_side, 1 - core))
    col_own = pick(col_side, core)

    front = parent_front.reshape(-1, B)
    mine_cols = lax.dynamic_index_in_dim(col_slots, core, 1, keepdims=False)
    mine_counts = lax.dynamic_index_in_dim(counts, core, 1, keepdims=False)
    out = extend(at, mine_counts, mine_cols, row_slots, front, row_side, row_other, col_own, col_other)
    return out.reshape(parent_front.shape)


def solution(mesh):
    rows, cols = AXES[:2], AXES[2:]
    split_mesh = Mesh(mesh.devices.reshape(SIZES), AXES)
    front = P(None, rows, None, None, cols, None)
    return jax.shard_map(
        per_device,
        mesh=split_mesh,
        in_specs=(P(None, AXES, None), P(rows, cols, None, None), P(), P(), front),
        out_specs=front,
        check_vma=False,
    )
```

```python
import functools

import jax
import jax.numpy as jnp
import numpy as np
from jax import lax
from jax.experimental import pallas as pl
from jax.experimental.pallas import tpu as pltpu
from jax.sharding import Mesh, PartitionSpec as P

F32 = jnp.float32
BF16 = jnp.bfloat16
B = 128
PW = 512
VMEM_BYTES = 56 << 20
STRIP = 32
AXES = ("yhi", "x", "ylo", "z", "core")
SIZES = (2, 4, 2, 4, 2)


def split(x):
    hi = x.astype(BF16)
    return hi, (x - hi.astype(F32)).astype(BF16)


def dot_t(x, y):
    return lax.dot_general(x, y, (((1,), (1,)), ((), ())), preferred_element_type=F32)


def dot3_t(xh, xl, yh, yl):
    return dot_t(jnp.concatenate([xh, xh, xl], axis=1), jnp.concatenate([yh, yl, yh], axis=1))


def leaf_inverse(block):
    lane = lax.broadcasted_iota(jnp.int32, (8, B), 1)
    sub = lax.broadcasted_iota(jnp.int32, (8, B), 0)
    rest = [block[8 * i : 8 * i + 8, :] for i in range(B // 8)]
    done = []
    for t in range(B // 8):
        lo = 8 * t
        cols = [[jnp.broadcast_to(x[:, lo + j : lo + j + 1], (8, B)) for x in rest] for j in range(8)]
        rel = lane - lo
        inside = (rel >= 0) & (rel < 8)
        rows = [jnp.where(inside, jnp.where(rel == sub, 1.0, 0.0), rest[0])]
        rows += [jnp.where(inside, 0.0, x) for x in rest[1:]]
        pivots = jnp.ones((8, B), F32)
        for j in range(8):
            pivot = jnp.broadcast_to(cols[j][0][j : j + 1, :], (8, B))
            pivots = jnp.where(sub == j, pivot, pivots)
            recip = 1.0 / pivot
            mult = [x * recip for x in cols[j]]
            mult[0] = jnp.where(sub > j, mult[0], 0.0)
            for jj in range(j + 1, 8):
                head = jnp.broadcast_to(cols[jj][0][j : j + 1, :], (8, B))
                cols[jj] = [x - m * head for x, m in zip(cols[jj], mult)]
            row = jnp.broadcast_to(rows[0][j : j + 1, :], (8, B))
            rows = [x - m * row for x, m in zip(rows, mult)]
        done.append(jnp.where(lane <= sub + lo, rows[0] * lax.rsqrt(pivots), 0.0))
        rest = rows[1:]
    return jnp.concatenate(done, axis=0)


def place_strips(at_ref, pieces, work):
    yhi, x, ylo, z, core = (at_ref[i] for i in range(5))
    y = yhi * 2 + ylo
    for ref, far, first in pieces:

        def strip(g, carry, ref=ref, far=far, first=first):
            mid, near = g // 4 + first, g % 4
            xx = (x - jnp.where(core == 0, mid, far)) & 3
            yy = (y - jnp.where(core == 0, far, mid)) & 3
            zz = (z - near) & 3
            row = ((yy // 2) * 4 + xx) * 8 + (yy % 2) * 4 + zz
            rows = pl.ds(pl.multiple_of(g * STRIP, STRIP), STRIP)
            to = pl.ds(pl.multiple_of(row * STRIP, STRIP), STRIP)
            work[to, :] = ref[rows, :].astype(F32)
            return carry

        lax.fori_loop(0, ref.shape[0] // STRIP, strip, 0)


def panel_kernel(s, where, at_ref, *refs):
    pieces, refs = refs[: len(where)], refs[len(where) :]
    prev = [(refs[2 * p], refs[2 * p + 1]) for p in range(s)]
    hi_ref, lo_ref, work, square = refs[2 * s :]
    n = work.shape[0]
    base = s * PW
    place_strips(at_ref, [(ref,) + place for ref, place in zip(pieces, where)], work)

    def load(pair, rows):
        return pair[0][rows, :], pair[1][rows, :]

    right = [load(pair, pl.ds(base, PW)) for pair in prev]

    def less_left(rb, out):
        first = 0 if rb >= s else rb

        def chunk(c, carry):
            rows = pl.ds(pl.multiple_of(rb * PW + c * 256, 256), 256)
            total = work[rows, :] if rb >= s else jnp.zeros((256, PW), F32)
            for p in range(first, s):
                total = total - dot3_t(*load(prev[p], rows), *right[p])
            out(c, rows, total)
            return carry

        lax.fori_loop(0, PW // 256, chunk, 0)

    def to_square(c, rows, total):
        square[pl.ds(pl.multiple_of(c * 256, 256), 256), :] = total

    less_left(s, to_square)
    eye = (lax.broadcasted_iota(jnp.int32, (B, B), 0) == lax.broadcasted_iota(jnp.int32, (B, B), 1)).astype(F32)

    def step(k, carry):
        cols = pl.ds(pl.multiple_of(k * B, B), B)
        inv = leaf_inverse(square[cols, cols])
        square[cols, cols] = eye
        qh, ql = split(dot3_t(*split(square[:, cols]), *split(inv)))
        hi_ref[pl.ds(base, PW), cols] = qh
        lo_ref[pl.ds(base, PW), cols] = ql
        for kk in range(PW // B - 1):

            @pl.when(k == kk)
            def _(kk=kk):
                width = PW - (kk + 1) * B
                at = pl.ds(kk * B, B)
                later = pl.ds((kk + 1) * B, width)
                below = pl.ds(base + (kk + 1) * B, width)
                square[at, later] = jnp.zeros((B, width), F32)
                yh, yl = hi_ref[below, at], lo_ref[below, at]
                qh, ql = hi_ref[pl.ds(base, PW), at], lo_ref[pl.ds(base, PW), at]
                square[:, later] = square[:, later] - dot3_t(qh, ql, yh, yl)
                hi_ref[below, at] = jnp.zeros((width, B), BF16)
                lo_ref[below, at] = jnp.zeros((width, B), BF16)

        return carry

    lax.fori_loop(0, PW // B, step, 0)
    vh, vl = hi_ref[pl.ds(base, PW), :], lo_ref[pl.ds(base, PW), :]
    stacked = jnp.concatenate([vh, vl, vh], axis=0)

    def to_out(c, rows, total):
        xh, xl = split(total)
        q = jnp.dot(jnp.concatenate([xh, xh, xl], axis=1), stacked, preferred_element_type=F32)
        hi_ref[rows, :], lo_ref[rows, :] = split(q)

    for rb in range(n // PW):
        if rb != s:
            less_left(rb, to_out)


def factor_panel(s, n, at, pieces, where, prev):
    flat = [x for pair in prev for x in pair]
    full = pl.BlockSpec(memory_space=pltpu.VMEM)
    out = jax.ShapeDtypeStruct((n, PW), BF16)
    return pl.pallas_call(
        functools.partial(panel_kernel, s, where),
        out_shape=(out, out),
        in_specs=[pl.BlockSpec(memory_space=pltpu.SMEM)] + [full] * (len(pieces) + len(flat)),
        out_specs=(full, full),
        scratch_shapes=[pltpu.VMEM((n, PW), F32), pltpu.VMEM((PW, PW), F32)],
        compiler_params=pltpu.CompilerParams(vmem_limit_bytes=VMEM_BYTES),
        cost_estimate=pl.CostEstimate(flops=30 * 10**9, bytes_accessed=10**7, transcendentals=0),
        name="factor_panel",
    )(at, *pieces, *flat)


def times_inverse(x, v_refs, store):
    for s in range(len(v_refs) // 2):
        vh, vl = v_refs[2 * s], v_refs[2 * s + 1]
        part = x[:, : (s + 1) * PW]
        both = jnp.concatenate([part, part], axis=1)
        v = jnp.concatenate([vh[...], vl[...]], axis=0)
        store(s, jnp.dot(both, v, preferred_element_type=F32).astype(BF16))


def v_specs(count):
    specs = []
    for s in range(count):
        spec = pl.BlockSpec(((s + 1) * PW, PW), lambda *_: (0, 0), pipeline_mode=pl.Buffered(1))
        specs += [spec, spec]
    return specs


def solve_kernel(count_ref, order_ref, x0_ref, x1_ref, *refs):
    out_ref = refs[-1]

    @pl.when(2 * pl.program_id(0) < count_ref[0])
    def _():
        def store(s, value):
            out_ref[:, s * PW : (s + 1) * PW] = value

        times_inverse(jnp.concatenate([x0_ref[0], x1_ref[0]], axis=0), refs[:-1], store)


def solve(x, count, order, panels):
    n = x.shape[2]
    flat = [v for pair in panels for v in pair]
    return pl.pallas_call(
        solve_kernel,
        grid_spec=pltpu.PrefetchScalarGridSpec(
            num_scalar_prefetch=2,
            grid=(4,),
            in_specs=[
                pl.BlockSpec((1, B, n), lambda g, c, o: (o[2 * g], 0, 0)),
                pl.BlockSpec((1, B, n), lambda g, c, o: (o[2 * g + 1], 0, 0)),
            ]
            + v_specs(len(panels)),
            out_specs=pl.BlockSpec((2 * B, n), lambda g, c, o: (g, 0)),
        ),
        out_shape=jax.ShapeDtypeStruct((8 * B, n), BF16),
        compiler_params=pltpu.CompilerParams(vmem_limit_bytes=VMEM_BYTES),
        cost_estimate=pl.CostEstimate(flops=12 * 10**9, bytes_accessed=2 * 10**7, transcendentals=0),
        name="solve",
    )(count, order, x, x, *flat)


def extend_kernel(at_ref, count_ref, col_ref, row_ref, front_ref, r0_ref, r1_ref, c0_ref, c1_ref, out_ref, prod):
    total = front_ref.shape[0]
    ylo, z = at_ref[2], at_ref[3]

    def fill(c, carry):
        rows = pl.ds(pl.multiple_of(c * 1024, 1024), 1024)
        out_ref[rows, :] = front_ref[rows, :].astype(F32)
        return carry

    lax.fori_loop(0, total // 1024, fill, 0)
    for a, (r_ref, c_ref) in enumerate(((r0_ref, c0_ref), (r1_ref, c1_ref))):
        count = count_ref[a]

        def pair(g, carry, a=a, r_ref=r_ref, c_ref=c_ref, count=count):
            right = c_ref[pl.ds(pl.multiple_of(g * 2 * B, 2 * B), 2 * B), :]

            def half(h, inner):
                rows = pl.ds(pl.multiple_of(h * 512, 512), 512)
                prod[rows, :] = dot_t(r_ref[rows, :], right)
                return inner

            lax.fori_loop(0, 2, half, 0)
            for m in range(2):

                @pl.when(2 * g + m < count)
                def _(m=m):
                    slot = col_ref[a, 2 * g + m]
                    for b in range(8):
                        block = ((ylo + b) & 1) * 4 + ((z - b // 2) & 3)
                        at = pl.ds(row_ref[a, block] * (8 * B) + slot, B, stride=8)
                        out_ref[at, :] = out_ref[at, :] - prod[b * B : (b + 1) * B, m * B : (m + 1) * B]

            return carry

        lax.fori_loop(0, (count + 1) // 2, pair, 0)


def extend(at, counts, col_slots, row_slots, front, r0, r1, c0, c1):
    smem = pl.BlockSpec(memory_space=pltpu.SMEM)
    vmem = pl.BlockSpec(memory_space=pltpu.VMEM)
    return pl.pallas_call(
        extend_kernel,
        out_shape=jax.ShapeDtypeStruct(front.shape, F32),
        in_specs=[smem] * 4 + [vmem] * 5,
        out_specs=vmem,
        scratch_shapes=[pltpu.VMEM((8 * B, 2 * B), F32)],
        compiler_params=pltpu.CompilerParams(vmem_limit_bytes=VMEM_BYTES),
        name="extend_add",
    )(at, counts, col_slots, row_slots, front, r0, r1, c0, c1)


def move(x, target):
    def flat(c):
        return int(np.ravel_multi_index(c, SIZES))

    pairs = [(flat(c), flat(target(*c))) for c in np.ndindex(*SIZES)]
    return lax.ppermute(x, AXES, pairs)


def step_z(by):
    return lambda yhi, x, ylo, z, core: (yhi, x, ylo, (z + by) % 4, core)


def step_x(by):
    return lambda yhi, x, ylo, z, core: (yhi, (x + by) % 4, ylo, z, core)


def step_y(by):
    def target(yhi, x, ylo, z, core):
        y = (yhi * 2 + ylo + by) % 4
        return (y // 2, x, y % 2, z, core)

    return target


def step_first(by):
    return lambda *c: (step_x(by) if c[4] == 0 else step_y(by))(*c)


def step_second(by):
    return lambda *c: (step_y(by) if c[4] == 0 else step_x(by))(*c)


def ring(x, step):
    return x, move(x, step(1)), move(x, step(2)), move(x, step(-1))


RING_PLACES = ((0, 0), (1, 0), (2, 0), (3, 0))


def ring_relay(x, step):
    half = x.shape[0] // 2
    back = move(x, step(1))
    ahead = move(x, step(-1))
    return x, back, move(back[:half], step(1)), move(ahead[half:], step(-1)), ahead


RELAY_PLACES = ((0, 0), (1, 0), (2, 0), (2, 2), (3, 0))


def after(x, done):
    return lax.optimization_barrier((x, done))


def swap(x):
    return move(x, lambda yhi, x, ylo, z, core: (yhi, x, ylo, z, 1 - core))


def to_row_group(yhi, x, ylo, z, core):
    i = z * 2 + core
    return (yhi, x, i // 4, i % 4, ylo)


def to_col_group(yhi, x, ylo, z, core):
    r, i = yhi * 4 + x, z * 2 + core
    return (i // 4, i % 4, r % 2, r // 2, ylo)


def pick(x, index):
    return lax.dynamic_index_in_dim(x, index, 0, keepdims=False)


def per_device(child_pivot, child_panel, child_map, panel_mask, parent_front):
    yhi, x, ylo, z, core = (lax.axis_index(name) for name in AXES)
    row = yhi * 4 + x
    y = yhi * 2 + ylo
    at = jnp.stack([yhi, x, ylo, z, core]).astype(jnp.int32)
    n = child_pivot.shape[2]
    np_ = n // PW

    other = swap(pick(child_pivot, 1 - core))
    own = pick(child_pivot, core)
    strip = jnp.where(core == 0, jnp.concatenate([own, other]), jnp.concatenate([other, own]))
    strip = strip.reshape(STRIP, np_, PW).transpose(1, 0, 2)

    def near(part, axis):
        return jnp.stack(ring(part, step_z), axis=axis)

    first = near(strip[0], 0)
    rest = near(strip[1:], 1)
    first = jnp.stack(ring(first, step_first)).reshape(16 * STRIP, PW)
    rest, first = after(rest, first)
    pieces = [ring_relay(first, step_second)]
    rest = jnp.stack(ring(rest, step_first), axis=1).reshape(np_ - 1, 16 * STRIP, PW)
    pieces += [ring(rest[s], step_second) for s in range(np_ - 1)]
    places = [RELAY_PLACES] + [RING_PLACES] * (np_ - 1)

    maps = child_map.reshape(2, 8, 8)
    maps = jnp.stack([pick(maps, core), pick(maps, 1 - core)])
    slots = maps // 8
    row_slots = lax.dynamic_index_in_dim(slots, row, 1, keepdims=False)
    by_col = lax.dynamic_slice_in_dim(slots, 2 * z, 2, axis=1)
    needed = by_col % 2 == ylo
    place = jnp.cumsum(needed.astype(jnp.int32), axis=2) - 1
    hit = (place[..., None, :] == jnp.arange(8)[:, None]) & needed[..., None, :]
    i = jnp.arange(8)
    dx = (x - i % 4)[None, :] % 4
    dy = (y - (i // 4)[None, :] * 2 - jnp.arange(2)[:, None]) % 4
    dx = jnp.broadcast_to(dx, dy.shape)
    where = jnp.where(core == 0, dy * 4 + dx, dx * 4 + dy)
    order = jnp.sum(jnp.where(hit[0], where[:, None, :], 0), axis=2).astype(jnp.int32)
    col_slots = jnp.sum(jnp.where(hit, (by_col // 2)[..., None, :], 0), axis=3).astype(jnp.int32)
    counts = jnp.sum(needed, axis=2).astype(jnp.int32)

    mine_cols = lax.dynamic_index_in_dim(col_slots, core, 1, keepdims=False)
    mine_counts = lax.dynamic_index_in_dim(counts, core, 1, keepdims=False)
    ask_near = (pick(counts[0], 1 - core)[None], pick(order, 1 - core))
    ask_own = (pick(counts[0], core)[None], pick(order, core))
    small = (mine_cols, mine_counts, row_slots, ask_near, ask_own)

    mask = pick(pick(panel_mask, ylo), row * 8 + z * 2 + core)
    kept = (child_panel.reshape(B, n // B, B) * mask.astype(BF16)[None, :, None]).reshape(B, n)
    (kept, small), rest = after((kept, small), rest)
    mine_cols, mine_counts, row_slots, ask_near, ask_own = small
    for_col = move(kept, to_col_group)
    for_row = move(kept, to_row_group)

    panels = [factor_panel(0, n, at, pieces[0], places[0], [])]
    (for_col, for_row), panels[0] = after((for_col, for_row), panels[0])
    for_col = jnp.stack(ring(for_col, step_first))
    for_row = jnp.stack([for_row, move(for_row, lambda yhi, x, ylo, z, core: (yhi, x, 1 - ylo, z, core))])
    panels.append(factor_panel(1, n, at, pieces[1], places[1], panels))
    (for_col, for_row), panels[1] = after((for_col, for_row), panels[1])
    for_col = ring(for_col, step_second)
    for_row = ring(for_row, step_z)
    for s in range(2, np_):
        panels.append(factor_panel(s, n, at, pieces[s], places[s], panels))
    col_panel = jnp.stack(for_col).reshape(16, B, n)
    row_panel = jnp.stack(for_row).reshape(8, B, n)

    col_other = swap(solve(col_panel, *ask_near, panels))
    row_side = solve(row_panel, jnp.full((1,), 8, jnp.int32), jnp.arange(8, dtype=jnp.int32), panels)
    row_other = swap(row_side)
    row_side, col_panel = after(row_side, col_panel)
    col_own = solve(col_panel, *ask_own, panels)

    front = parent_front.reshape(-1, B)
    out = extend(at, mine_counts, mine_cols, row_slots, front, row_side, row_other, col_own, col_other)
    return out.reshape(parent_front.shape)


def solution(mesh):
    rows, cols = AXES[:2], AXES[2:]
    split_mesh = Mesh(mesh.devices.reshape(SIZES), AXES)
    front = P(None, rows, None, None, cols, None)
    return jax.shard_map(
        per_device,
        mesh=split_mesh,
        in_specs=(P(None, AXES, None), P(rows, cols, None, None), P(), P(), front),
        out_specs=front,
        check_vma=False,
    )
```

```python
import functools

import jax
import jax.numpy as jnp
import numpy as np
from jax import lax
from jax.experimental import pallas as pl
from jax.experimental.pallas import tpu as pltpu
from jax.sharding import Mesh, PartitionSpec as P

F32 = jnp.float32
BF16 = jnp.bfloat16
B = 128
PW = 512
VMEM_BYTES = 56 << 20
STRIP = 32
AXES = ("yhi", "x", "ylo", "z", "core")
SIZES = (2, 4, 2, 4, 2)


def split(x):
    hi = x.astype(BF16)
    return hi, (x - hi.astype(F32)).astype(BF16)


def dot_t(x, y):
    return lax.dot_general(x, y, (((1,), (1,)), ((), ())), preferred_element_type=F32)


def dot3_t(xh, xl, yh, yl):
    return dot_t(jnp.concatenate([xh, xh, xl], axis=1), jnp.concatenate([yh, yl, yh], axis=1))


def leaf_inverse(block):
    lane = lax.broadcasted_iota(jnp.int32, (8, B), 1)
    sub = lax.broadcasted_iota(jnp.int32, (8, B), 0)
    groups = B // 8
    rows = [block[8 * i : 8 * i + 8, :] for i in range(groups)]

    def row_of(x, j):
        return jnp.broadcast_to(x[j : j + 1, :], (8, B))

    def col_of(x, j):
        return jnp.broadcast_to(x[:, j : j + 1], (8, B))

    def total(p):
        return ((p[0] + p[1]) + (p[2] + p[3])) + ((p[4] + p[5]) + (p[6] + p[7]))

    done = []
    cols = [col_of(rows[0], j) for j in range(8)]
    for t in range(groups):
        lo = 8 * t
        rel = lane - lo
        inside = (rel >= 0) & (rel < 8)
        last = t == groups - 1
        if not last:
            ahead = [col_of(rows[t], lo + 8 + j) for j in range(8)]
            below = [col_of(rows[t + 1], lo + 8 + j) for j in range(8)]
            left = [col_of(rows[t + 1], lo + j) for j in range(8)]
        half = jnp.where(inside, jnp.where(rel == sub, 1.0, 0.0), rows[t])
        full = half
        pivots = jnp.ones((8, B), F32)
        recips = jnp.ones((8, B), F32)
        for j in range(8):
            pivot = row_of(cols[j], j)
            recip = pltpu.reciprocal(pivot, approx=True)
            pivots = jnp.where(sub == j, pivot, pivots)
            recips = jnp.where(sub == j, recip, recips)
            mult = jnp.where(sub != j, cols[j], 0.0) * recip
            for jj in range(j + 1, 8):
                cols[jj] = cols[jj] - mult * row_of(cols[jj], j)
            row = row_of(half, j)
            half = half - jnp.where(sub > j, mult, 0.0) * row
            full = full - mult * row
            if not last:
                ahead = [c - mult * row_of(c, j) for c in ahead]
        full = full * recips
        done.append(jnp.where(lane <= sub + lo, half * lax.rsqrt(pivots), 0.0))
        if last:
            break
        ahead = [c * recips for c in ahead]
        cols = [b - total([left[j] * row_of(c, j) for j in range(8)]) for b, c in zip(below, ahead)]
        rows[t + 1] = jnp.where(inside, 0.0, rows[t + 1]) - total([left[j] * row_of(full, j) for j in range(8)])
        if t + 2 < groups:
            lh, ll = split(jnp.concatenate([jnp.where(inside, r, 0.0) for r in rows[t + 2 :]], axis=0))
            zero = jnp.zeros((8, B), F32)
            fh, fl = split(jnp.concatenate([full if i == t else zero for i in range(groups)], axis=0))
            less = jnp.dot(
                jnp.concatenate([lh, lh, ll], axis=1),
                jnp.concatenate([fh, fl, fh], axis=0),
                preferred_element_type=F32,
            )
            for i in range(t + 2, groups):
                rows[i] = jnp.where(inside, 0.0, rows[i]) - less[8 * (i - t - 2) : 8 * (i - t - 1)]
    return jnp.concatenate(done, axis=0)


def place_strips(at_ref, pieces, work):
    yhi, x, ylo, z, core = (at_ref[i] for i in range(5))
    y = yhi * 2 + ylo
    for far, ref in enumerate(pieces):

        def strip(g, carry, ref=ref, far=far):
            mid, near = g // 4, g % 4
            xx = (x - jnp.where(core == 0, mid, far)) & 3
            yy = (y - jnp.where(core == 0, far, mid)) & 3
            zz = (z - near) & 3
            row = ((yy // 2) * 4 + xx) * 8 + (yy % 2) * 4 + zz
            rows = pl.ds(pl.multiple_of(g * STRIP, STRIP), STRIP)
            to = pl.ds(pl.multiple_of(row * STRIP, STRIP), STRIP)
            work[to, :] = ref[0, rows, :].astype(F32)
            return carry

        lax.fori_loop(0, ref.shape[1] // STRIP, strip, 0)


def panel_kernel(s, at_ref, *refs):
    pieces, refs = refs[:4], refs[4:]
    prev = [(refs[2 * p], refs[2 * p + 1]) for p in range(s)]
    hi_ref, lo_ref, work, square = refs[2 * s :]
    n = work.shape[0]
    base = s * PW
    place_strips(at_ref, pieces, work)

    def load(pair, rows):
        return pair[0][rows, :], pair[1][rows, :]

    right = [load(pair, pl.ds(base, PW)) for pair in prev]

    def left(rows, p):
        return dot3_t(*load(prev[p], rows), *right[p])

    def own_rows(c, carry):
        rows = pl.ds(pl.multiple_of(base + c * 256, 256), 256)
        total = work[rows, :]
        for p in range(s):
            total = total - left(rows, p)
        square[pl.ds(pl.multiple_of(c * 256, 256), 256), :] = total
        return carry

    lax.fori_loop(0, PW // 256, own_rows, 0)

    def other_rows(k):
        if s == 0:
            return
        count = (n - PW) // (4 * B)
        at = [k * ((n - PW) // 4) + i * B for i in range(count)]
        at = [jnp.where(row < base, row, row + PW) for row in at]
        rows = [pl.ds(pl.multiple_of(row, B), B) for row in at]
        total = jnp.concatenate([jnp.where(row > base, work[r, :], 0.0) for row, r in zip(at, rows)], axis=0)
        for p in range(s):
            part = [load(prev[p], r) for r in rows]
            product = dot3_t(*[jnp.concatenate(half, axis=0) for half in zip(*part)], *right[p])
            use = [(row > base) | (row < (p + 1) * PW) for row in at]
            use = [jnp.broadcast_to(u.astype(F32), (B, PW)) for u in use]
            total = total - product * jnp.concatenate(use, axis=0)
        for i, r in enumerate(rows):
            work[r, :] = total[i * B : (i + 1) * B]

    eye = (lax.broadcasted_iota(jnp.int32, (B, B), 0) == lax.broadcasted_iota(jnp.int32, (B, B), 1)).astype(F32)

    def step(k, carry):
        cols = pl.ds(pl.multiple_of(k * B, B), B)
        block = square[cols, cols]
        other_rows(k)
        inv = leaf_inverse(block)
        square[cols, cols] = eye
        qh, ql = split(dot3_t(*split(square[:, cols]), *split(inv)))
        hi_ref[pl.ds(base, PW), cols] = qh
        lo_ref[pl.ds(base, PW), cols] = ql
        for kk in range(PW // B - 1):

            @pl.when(k == kk)
            def _(kk=kk):
                width = PW - (kk + 1) * B
                at = pl.ds(kk * B, B)
                later = pl.ds((kk + 1) * B, width)
                below = pl.ds(base + (kk + 1) * B, width)
                square[at, later] = jnp.zeros((B, width), F32)
                yh, yl = hi_ref[below, at], lo_ref[below, at]
                qh, ql = hi_ref[pl.ds(base, PW), at], lo_ref[pl.ds(base, PW), at]
                square[:, later] = square[:, later] - dot3_t(qh, ql, yh, yl)
                hi_ref[below, at] = jnp.zeros((width, B), BF16)
                lo_ref[below, at] = jnp.zeros((width, B), BF16)

        return carry

    lax.fori_loop(0, PW // B, step, 0)
    vh, vl = hi_ref[pl.ds(base, PW), :], lo_ref[pl.ds(base, PW), :]
    stacked = jnp.concatenate([vh, vl, vh], axis=0)
    for rb in range(n // PW):
        if rb != s:

            def rest(c, carry, rb=rb):
                rows = pl.ds(pl.multiple_of(rb * PW + c * 256, 256), 256)
                xh, xl = split(work[rows, :])
                q = jnp.dot(jnp.concatenate([xh, xh, xl], axis=1), stacked, preferred_element_type=F32)
                hi_ref[rows, :], lo_ref[rows, :] = split(q)
                return carry

            lax.fori_loop(0, PW // 256, rest, 0)


def factor_panel(s, n, at, pieces, prev):
    flat = [x for pair in prev for x in pair]
    full = pl.BlockSpec(memory_space=pltpu.VMEM)
    out = jax.ShapeDtypeStruct((n, PW), BF16)
    return pl.pallas_call(
        functools.partial(panel_kernel, s),
        grid=(1,),
        out_shape=(out, out),
        in_specs=[pl.BlockSpec(memory_space=pltpu.SMEM)]
        + [
            pl.BlockSpec((1,) + x.shape[1:], lambda g, i=i: (i, 0, 0), pipeline_mode=pl.Buffered(1)) for x, i in pieces
        ]
        + [full] * len(flat),
        out_specs=(full, full),
        scratch_shapes=[pltpu.VMEM((n, PW), F32), pltpu.VMEM((PW, PW), F32)],
        compiler_params=pltpu.CompilerParams(vmem_limit_bytes=VMEM_BYTES),
        cost_estimate=pl.CostEstimate(flops=30 * 10**9, bytes_accessed=10**7, transcendentals=0),
        name="factor_panel",
    )(at, *[x for x, _ in pieces], *flat)


def times_inverse(x, v_refs, store):
    for s in range(len(v_refs) // 2):
        vh, vl = v_refs[2 * s], v_refs[2 * s + 1]
        part = x[:, : (s + 1) * PW]
        both = jnp.concatenate([part, part], axis=1)
        v = jnp.concatenate([vh[...], vl[...]], axis=0)
        store(s, jnp.dot(both, v, preferred_element_type=F32).astype(BF16))


def v_specs(count):
    specs = []
    for s in range(count):
        spec = pl.BlockSpec(((s + 1) * PW, PW), lambda *_: (0, 0), pipeline_mode=pl.Buffered(1))
        specs += [spec, spec]
    return specs


def solve_kernel(count_ref, order_ref, x0_ref, x1_ref, *refs):
    out_ref = refs[-1]

    @pl.when(2 * pl.program_id(0) < count_ref[0])
    def _():
        def store(s, value):
            out_ref[:, s * PW : (s + 1) * PW] = value

        times_inverse(jnp.concatenate([x0_ref[0], x1_ref[0]], axis=0), refs[:-1], store)


def solve(x, count, order, panels):
    n = x.shape[2]
    flat = [v for pair in panels for v in pair]
    return pl.pallas_call(
        solve_kernel,
        grid_spec=pltpu.PrefetchScalarGridSpec(
            num_scalar_prefetch=2,
            grid=(4,),
            in_specs=[
                pl.BlockSpec((1, B, n), lambda g, c, o: (o[2 * g], 0, 0)),
                pl.BlockSpec((1, B, n), lambda g, c, o: (o[2 * g + 1], 0, 0)),
            ]
            + v_specs(len(panels)),
            out_specs=pl.BlockSpec((2 * B, n), lambda g, c, o: (g, 0)),
        ),
        out_shape=jax.ShapeDtypeStruct((8 * B, n), BF16),
        compiler_params=pltpu.CompilerParams(vmem_limit_bytes=VMEM_BYTES),
        cost_estimate=pl.CostEstimate(flops=12 * 10**9, bytes_accessed=2 * 10**7, transcendentals=0),
        name="solve",
    )(count, order, x, x, *flat)


def extend_kernel(count_ref, col_ref, row_ref, front_ref, r0_ref, r1_ref, c0_ref, c1_ref, out_ref, prod):
    total = front_ref.shape[0]

    def fill(c, carry):
        rows = pl.ds(pl.multiple_of(c * 1024, 1024), 1024)
        out_ref[rows, :] = front_ref[rows, :].astype(F32)
        return carry

    lax.fori_loop(0, total // 1024, fill, 0)
    for a, (r_ref, c_ref) in enumerate(((r0_ref, c0_ref), (r1_ref, c1_ref))):
        count = count_ref[a]

        def pair(g, carry, a=a, r_ref=r_ref, c_ref=c_ref, count=count):
            right = c_ref[pl.ds(pl.multiple_of(g * 2 * B, 2 * B), 2 * B), :]

            def half(h, inner):
                rows = pl.ds(pl.multiple_of(h * 512, 512), 512)
                prod[rows, :] = dot_t(r_ref[rows, :], right)
                return inner

            lax.fori_loop(0, 2, half, 0)
            for m in range(2):

                @pl.when(2 * g + m < count)
                def _(m=m):
                    slot = col_ref[a, 2 * g + m]
                    for b in range(8):
                        at = pl.ds(row_ref[a, b] * (8 * B) + slot, B, stride=8)
                        out_ref[at, :] = out_ref[at, :] - prod[b * B : (b + 1) * B, m * B : (m + 1) * B]

            return carry

        lax.fori_loop(0, (count + 1) // 2, pair, 0)


def extend(counts, col_slots, row_slots, front, r0, r1, c0, c1):
    smem = pl.BlockSpec(memory_space=pltpu.SMEM)
    vmem = pl.BlockSpec(memory_space=pltpu.VMEM)
    return pl.pallas_call(
        extend_kernel,
        out_shape=jax.ShapeDtypeStruct(front.shape, F32),
        in_specs=[smem] * 3 + [vmem] * 5,
        out_specs=vmem,
        scratch_shapes=[pltpu.VMEM((8 * B, 2 * B), F32)],
        compiler_params=pltpu.CompilerParams(vmem_limit_bytes=VMEM_BYTES),
        name="extend_add",
    )(counts, col_slots, row_slots, front, r0, r1, c0, c1)


def move(x, target):
    def flat(c):
        return int(np.ravel_multi_index(c, SIZES))

    pairs = [(flat(c), flat(target(*c))) for c in np.ndindex(*SIZES)]
    return lax.ppermute(x, AXES, pairs)


def step_z(by):
    return lambda yhi, x, ylo, z, core: (yhi, x, ylo, (z + by) % 4, core)


def step_x(by):
    return lambda yhi, x, ylo, z, core: (yhi, (x + by) % 4, ylo, z, core)


def step_y(by):
    def target(yhi, x, ylo, z, core):
        y = (yhi * 2 + ylo + by) % 4
        return (y // 2, x, y % 2, z, core)

    return target


def step_first(by):
    return lambda *c: (step_x(by) if c[4] == 0 else step_y(by))(*c)


def step_second(by):
    return lambda *c: (step_y(by) if c[4] == 0 else step_x(by))(*c)


def ring(x, step):
    return x, move(x, step(1)), move(x, step(2)), move(x, step(-1))


def after(x, done):
    return lax.optimization_barrier((x, done))


def axis_groups(stage):
    groups = {}
    for c in np.ndindex(*SIZES):
        yhi, x, ylo, z, core = c
        along_x = core == stage
        key = (core, z, yhi, ylo) if along_x else (core, z, x)
        groups.setdefault(key, []).append((x if along_x else yhi * 2 + ylo, int(np.ravel_multi_index(c, SIZES))))
    return [[device for _, device in sorted(group)] for group in groups.values()]


def swap(x):
    return move(x, lambda yhi, x, ylo, z, core: (yhi, x, ylo, z, 1 - core))


def to_row_group(yhi, x, ylo, z, core):
    i = z * 2 + core
    return (yhi, x, i // 4, i % 4, ylo)


def to_col_group(yhi, x, ylo, z, core):
    r, i = yhi * 4 + x, z * 2 + core
    return (i // 4, i % 4, r % 2, r // 2, ylo)


def pick(x, index):
    return lax.dynamic_index_in_dim(x, index, 0, keepdims=False)


def per_device(child_pivot, child_panel, child_map, panel_mask, parent_front):
    yhi, x, ylo, z, core = (lax.axis_index(name) for name in AXES)
    row = yhi * 4 + x
    y = yhi * 2 + ylo
    at = jnp.stack([yhi, x, ylo, z, core]).astype(jnp.int32)
    n = child_pivot.shape[2]
    np_ = n // PW

    other = swap(pick(child_pivot, 1 - core))
    own = pick(child_pivot, core)
    strip = jnp.where(core == 0, jnp.concatenate([own, other]), jnp.concatenate([other, own]))
    strip = strip.reshape(STRIP, np_, PW).transpose(1, 0, 2)

    def plane(part):
        part = jnp.stack(ring(part, step_z), axis=1)
        return jnp.stack(ring(part, step_first), axis=1).reshape(2, 16 * STRIP, PW)

    mask = pick(pick(panel_mask, ylo), row * 8 + z * 2 + core)
    kept = (child_panel.reshape(B, n // B, B) * mask.astype(BF16)[None, :, None]).reshape(B, n)
    for_row = move(kept, to_row_group)
    for_col = move(kept, to_col_group)
    first = plane(strip[:2])
    first, (for_row, for_col) = after(first, (for_row, for_col))
    row_panel = lax.all_gather(for_row, ("ylo", "z"), axis=0)
    back, ahead = move(first, step_second(1)), move(first, step_second(-1))
    far = move(back[:1], step_second(1)), move(ahead[1:], step_second(-1))
    rest = plane(after(strip[2:], first)[0])

    maps = child_map.reshape(2, 8, 8)
    maps = jnp.stack([pick(maps, core), pick(maps, 1 - core)])
    slots = maps // 8
    row_slots = lax.dynamic_index_in_dim(slots, row, 1, keepdims=False)
    by_col = lax.dynamic_slice_in_dim(slots, 2 * z, 2, axis=1)
    needed = by_col % 2 == ylo
    place = jnp.cumsum(needed.astype(jnp.int32), axis=2) - 1
    hit = (place[..., None, :] == jnp.arange(8)[:, None]) & needed[..., None, :]
    i = jnp.arange(8)
    x_of = jnp.broadcast_to(i % 4, (2, 8))
    y_of = (i // 4)[None, :] * 2 + jnp.arange(2)[:, None]
    where = jnp.where(core == 0, y_of * 4 + x_of, x_of * 4 + y_of)
    order = jnp.sum(jnp.where(hit[0], where[:, None, :], 0), axis=2).astype(jnp.int32)
    col_slots = jnp.sum(jnp.where(hit, (by_col // 2)[..., None, :], 0), axis=3).astype(jnp.int32)
    counts = jnp.sum(needed, axis=2).astype(jnp.int32)

    mine_cols = lax.dynamic_index_in_dim(col_slots, core, 1, keepdims=False)
    mine_counts = lax.dynamic_index_in_dim(counts, core, 1, keepdims=False)
    ask_near = (pick(counts[0], 1 - core)[None], pick(order, 1 - core))
    ask_own = (pick(counts[0], core)[None], pick(order, core))
    small = (mine_cols, mine_counts, row_slots, ask_near, ask_own)

    (small, rest, row_panel), arrived = after((small, rest, row_panel), (back, ahead) + far)
    mine_cols, mine_counts, row_slots, ask_near, ask_own = small
    back, ahead, *far = arrived
    rest = ring(rest, step_second)

    panels = [factor_panel(0, n, at, [(first, 0), (back, 0), (far[0], 0), (ahead, 0)], [])]
    for_col, panels[0] = after(for_col, panels[0])
    for_col = lax.all_gather(for_col, AXES, axis=0, axis_index_groups=axis_groups(0))
    panels.append(factor_panel(1, n, at, [(first, 1), (back, 1), (far[1], 0), (ahead, 1)], panels))
    for_col, panels[1] = after(for_col, panels[1])
    for_col = lax.all_gather(for_col, AXES, axis=0, axis_index_groups=axis_groups(1))
    for s in range(2, np_):
        panels.append(factor_panel(s, n, at, [(x, s - 2) for x in rest], panels))
    col_panel = for_col.reshape(16, B, n)

    row_side = solve(row_panel, jnp.full((1,), 8, jnp.int32), jnp.arange(8, dtype=jnp.int32), panels)
    row_other = swap(row_side)
    row_side, col_panel = after(row_side, col_panel)
    col_other = solve(col_panel, *ask_near, panels)
    col_panel, col_other = after(col_panel, col_other)
    col_other = swap(col_other)
    col_own = solve(col_panel, *ask_own, panels)

    front = parent_front.reshape(-1, B)
    out = extend(mine_counts, mine_cols, row_slots, front, row_side, row_other, col_own, col_other)
    return out.reshape(parent_front.shape)


def solution(mesh):
    rows, cols = AXES[:2], AXES[2:]
    split_mesh = Mesh(mesh.devices.reshape(SIZES), AXES)
    front = P(None, rows, None, None, cols, None)
    return jax.shard_map(
        per_device,
        mesh=split_mesh,
        in_specs=(P(None, AXES, None), P(rows, cols, None, None), P(), P(), front),
        out_specs=front,
        check_vma=False,
    )
```

```python
import functools

import jax
import jax.numpy as jnp
import numpy as np
from jax import lax
from jax.experimental import pallas as pl
from jax.experimental.pallas import tpu as pltpu
from jax.sharding import Mesh, PartitionSpec as P

F32 = jnp.float32
BF16 = jnp.bfloat16
B = 128
PW = 512
VMEM_BYTES = 56 << 20
STRIP = 32
AXES = ("yhi", "x", "ylo", "z", "core")
SIZES = (2, 4, 2, 4, 2)


def split(x):
    hi = x.astype(BF16)
    return hi, (x - hi.astype(F32)).astype(BF16)


def dot_t(x, y):
    return lax.dot_general(x, y, (((1,), (1,)), ((), ())), preferred_element_type=F32)


def dot3_t(xh, xl, yh, yl):
    return dot_t(jnp.concatenate([xh, xh, xl], axis=1), jnp.concatenate([yh, yl, yh], axis=1))


def leaf_inverse(block):
    lane = lax.broadcasted_iota(jnp.int32, (8, B), 1)
    sub = lax.broadcasted_iota(jnp.int32, (8, B), 0)
    groups = B // 8
    rows = [block[8 * i : 8 * i + 8, :] for i in range(groups)]

    def row_of(x, j):
        return jnp.broadcast_to(x[j : j + 1, :], (8, B))

    def col_of(x, j):
        return jnp.broadcast_to(x[:, j : j + 1], (8, B))

    def total(p):
        return ((p[0] + p[1]) + (p[2] + p[3])) + ((p[4] + p[5]) + (p[6] + p[7]))

    done = []
    cols = [col_of(rows[0], j) for j in range(8)]
    for t in range(groups):
        lo = 8 * t
        rel = lane - lo
        inside = (rel >= 0) & (rel < 8)
        last = t == groups - 1
        if not last:
            ahead = [col_of(rows[t], lo + 8 + j) for j in range(8)]
            below = [col_of(rows[t + 1], lo + 8 + j) for j in range(8)]
            left = [col_of(rows[t + 1], lo + j) for j in range(8)]
        half = jnp.where(inside, jnp.where(rel == sub, 1.0, 0.0), rows[t])
        full = half
        pivots = jnp.ones((8, B), F32)
        recips = jnp.ones((8, B), F32)
        for j in range(8):
            pivot = row_of(cols[j], j)
            recip = pltpu.reciprocal(pivot, approx=True)
            pivots = jnp.where(sub == j, pivot, pivots)
            recips = jnp.where(sub == j, recip, recips)
            mult = jnp.where(sub != j, cols[j], 0.0) * recip
            for jj in range(j + 1, 8):
                cols[jj] = cols[jj] - mult * row_of(cols[jj], j)
            row = row_of(half, j)
            half = half - jnp.where(sub > j, mult, 0.0) * row
            full = full - mult * row
            if not last:
                ahead = [c - mult * row_of(c, j) for c in ahead]
        full = full * recips
        done.append(jnp.where(lane <= sub + lo, half * lax.rsqrt(pivots), 0.0))
        if last:
            break
        ahead = [c * recips for c in ahead]
        cols = [b - total([left[j] * row_of(c, j) for j in range(8)]) for b, c in zip(below, ahead)]
        rows[t + 1] = jnp.where(inside, 0.0, rows[t + 1]) - total([left[j] * row_of(full, j) for j in range(8)])
        if t + 2 < groups:
            lh, ll = split(jnp.concatenate([jnp.where(inside, r, 0.0) for r in rows[t + 2 :]], axis=0))
            zero = jnp.zeros((8, B), F32)
            fh, fl = split(jnp.concatenate([full if i == t else zero for i in range(groups)], axis=0))
            less = jnp.dot(
                jnp.concatenate([lh, lh, ll], axis=1),
                jnp.concatenate([fh, fl, fh], axis=0),
                preferred_element_type=F32,
            )
            for i in range(t + 2, groups):
                rows[i] = jnp.where(inside, 0.0, rows[i]) - less[8 * (i - t - 2) : 8 * (i - t - 1)]
    return jnp.concatenate(done, axis=0)


def place_strips(at_ref, pieces, work):
    yhi, x, ylo, z, core = (at_ref[i] for i in range(5))
    y = yhi * 2 + ylo
    for far, ref in enumerate(pieces):

        def strip(g, carry, ref=ref, far=far):
            mid, near = g // 4, g % 4
            xx = (x - jnp.where(core == 0, mid, far)) & 3
            yy = (y - jnp.where(core == 0, far, mid)) & 3
            zz = (z - near) & 3
            row = ((yy // 2) * 4 + xx) * 8 + (yy % 2) * 4 + zz
            rows = pl.ds(pl.multiple_of(g * STRIP, STRIP), STRIP)
            to = pl.ds(pl.multiple_of(row * STRIP, STRIP), STRIP)
            work[to, :] = ref[0, rows, :].astype(F32)
            return carry

        lax.fori_loop(0, ref.shape[1] // STRIP, strip, 0)


def panel_kernel(s, at_ref, *refs):
    pieces, refs = refs[:4], refs[4:]
    prev = [(refs[2 * p], refs[2 * p + 1]) for p in range(s)]
    hi_ref, lo_ref, work, square = refs[2 * s :]
    n = work.shape[0]
    base = s * PW
    place_strips(at_ref, pieces, work)

    def load(pair, rows):
        return pair[0][rows, :], pair[1][rows, :]

    right = [load(pair, pl.ds(base, PW)) for pair in prev]

    def left(rows, p):
        return dot3_t(*load(prev[p], rows), *right[p])

    def own_rows(c, carry):
        rows = pl.ds(pl.multiple_of(base + c * 256, 256), 256)
        total = work[rows, :]
        for p in range(s):
            total = total - left(rows, p)
        square[pl.ds(pl.multiple_of(c * 256, 256), 256), :] = total
        return carry

    lax.fori_loop(0, PW // 256, own_rows, 0)

    def other_rows(k):
        if s == 0:
            return
        count = (n - PW) // (4 * B)
        at = [k * ((n - PW) // 4) + i * B for i in range(count)]
        at = [jnp.where(row < base, row, row + PW) for row in at]
        rows = [pl.ds(pl.multiple_of(row, B), B) for row in at]
        total = jnp.concatenate([jnp.where(row > base, work[r, :], 0.0) for row, r in zip(at, rows)], axis=0)
        for p in range(s):
            part = [load(prev[p], r) for r in rows]
            product = dot3_t(*[jnp.concatenate(half, axis=0) for half in zip(*part)], *right[p])
            use = [(row > base) | (row < (p + 1) * PW) for row in at]
            use = [jnp.broadcast_to(u.astype(F32), (B, PW)) for u in use]
            total = total - product * jnp.concatenate(use, axis=0)
        for i, r in enumerate(rows):
            work[r, :] = total[i * B : (i + 1) * B]

    eye = (lax.broadcasted_iota(jnp.int32, (B, B), 0) == lax.broadcasted_iota(jnp.int32, (B, B), 1)).astype(F32)

    def step(k, carry):
        cols = pl.ds(pl.multiple_of(k * B, B), B)
        block = square[cols, cols]
        other_rows(k)
        inv = leaf_inverse(block)
        square[cols, cols] = eye
        qh, ql = split(dot3_t(*split(square[:, cols]), *split(inv)))
        hi_ref[pl.ds(base, PW), cols] = qh
        lo_ref[pl.ds(base, PW), cols] = ql
        for kk in range(PW // B - 1):

            @pl.when(k == kk)
            def _(kk=kk):
                width = PW - (kk + 1) * B
                at = pl.ds(kk * B, B)
                later = pl.ds((kk + 1) * B, width)
                below = pl.ds(base + (kk + 1) * B, width)
                square[at, later] = jnp.zeros((B, width), F32)
                yh, yl = hi_ref[below, at], lo_ref[below, at]
                qh, ql = hi_ref[pl.ds(base, PW), at], lo_ref[pl.ds(base, PW), at]
                square[:, later] = square[:, later] - dot3_t(qh, ql, yh, yl)
                hi_ref[below, at] = jnp.zeros((width, B), BF16)
                lo_ref[below, at] = jnp.zeros((width, B), BF16)

        return carry

    lax.fori_loop(0, PW // B, step, 0)
    vh, vl = hi_ref[pl.ds(base, PW), :], lo_ref[pl.ds(base, PW), :]
    stacked = jnp.concatenate([vh, vl, vh], axis=0)
    for rb in range(n // PW):
        if rb != s:

            def rest(c, carry, rb=rb):
                rows = pl.ds(pl.multiple_of(rb * PW + c * 256, 256), 256)
                xh, xl = split(work[rows, :])
                q = jnp.dot(jnp.concatenate([xh, xh, xl], axis=1), stacked, preferred_element_type=F32)
                hi_ref[rows, :], lo_ref[rows, :] = split(q)
                return carry

            lax.fori_loop(0, PW // 256, rest, 0)


def factor_panel(s, n, at, pieces, prev):
    flat = [x for pair in prev for x in pair]
    full = pl.BlockSpec(memory_space=pltpu.VMEM)
    out = jax.ShapeDtypeStruct((n, PW), BF16)
    return pl.pallas_call(
        functools.partial(panel_kernel, s),
        grid=(1,),
        out_shape=(out, out),
        in_specs=[pl.BlockSpec(memory_space=pltpu.SMEM)]
        + [
            pl.BlockSpec((1,) + x.shape[1:], lambda g, i=i: (i, 0, 0), pipeline_mode=pl.Buffered(1)) for x, i in pieces
        ]
        + [full] * len(flat),
        out_specs=(full, full),
        scratch_shapes=[pltpu.VMEM((n, PW), F32), pltpu.VMEM((PW, PW), F32)],
        compiler_params=pltpu.CompilerParams(vmem_limit_bytes=VMEM_BYTES),
        cost_estimate=pl.CostEstimate(flops=30 * 10**9, bytes_accessed=10**7, transcendentals=0),
        name="factor_panel",
    )(at, *[x for x, _ in pieces], *flat)


def times_inverse(x, v_refs, store):
    for s in range(len(v_refs) // 2):
        vh, vl = v_refs[2 * s], v_refs[2 * s + 1]
        part = x[:, : (s + 1) * PW]
        both = jnp.concatenate([part, part], axis=1)
        v = jnp.concatenate([vh[...], vl[...]], axis=0)
        store(s, jnp.dot(both, v, preferred_element_type=F32).astype(BF16))


def v_specs(count):
    specs = []
    for s in range(count):
        spec = pl.BlockSpec(((s + 1) * PW, PW), lambda *_: (0, 0), pipeline_mode=pl.Buffered(1))
        specs += [spec, spec]
    return specs


def solve_kernel(count_ref, order_ref, x0_ref, x1_ref, *refs):
    out_ref = refs[-1]

    @pl.when(2 * pl.program_id(0) < count_ref[0])
    def _():
        def store(s, value):
            out_ref[:, s * PW : (s + 1) * PW] = value

        times_inverse(jnp.concatenate([x0_ref[0], x1_ref[0]], axis=0), refs[:-1], store)


def solve(x, count, order, panels):
    n = x.shape[2]
    flat = [v for pair in panels for v in pair]
    return pl.pallas_call(
        solve_kernel,
        grid_spec=pltpu.PrefetchScalarGridSpec(
            num_scalar_prefetch=2,
            grid=(4,),
            in_specs=[
                pl.BlockSpec((1, B, n), lambda g, c, o: (o[2 * g], 0, 0)),
                pl.BlockSpec((1, B, n), lambda g, c, o: (o[2 * g + 1], 0, 0)),
            ]
            + v_specs(len(panels)),
            out_specs=pl.BlockSpec((2 * B, n), lambda g, c, o: (g, 0)),
        ),
        out_shape=jax.ShapeDtypeStruct((8 * B, n), BF16),
        compiler_params=pltpu.CompilerParams(vmem_limit_bytes=VMEM_BYTES),
        cost_estimate=pl.CostEstimate(flops=12 * 10**9, bytes_accessed=2 * 10**7, transcendentals=0),
        name="solve",
    )(count, order, x, x, *flat)


def extend_kernel(count_ref, col_ref, row_ref, front_ref, r0_ref, r1_ref, c0_ref, c1_ref, out_ref, prod):
    total = front_ref.shape[0]

    def fill(c, carry):
        rows = pl.ds(pl.multiple_of(c * 1024, 1024), 1024)
        out_ref[rows, :] = front_ref[rows, :].astype(F32)
        return carry

    lax.fori_loop(0, total // 1024, fill, 0)
    for a, (r_ref, c_ref) in enumerate(((r0_ref, c0_ref), (r1_ref, c1_ref))):
        count = count_ref[a]

        def pair(g, carry, a=a, r_ref=r_ref, c_ref=c_ref, count=count):
            right = c_ref[pl.ds(pl.multiple_of(g * 2 * B, 2 * B), 2 * B), :]

            def half(h, inner):
                rows = pl.ds(pl.multiple_of(h * 512, 512), 512)
                prod[rows, :] = dot_t(r_ref[rows, :], right)
                return inner

            lax.fori_loop(0, 2, half, 0)
            for m in range(2):

                @pl.when(2 * g + m < count)
                def _(m=m):
                    slot = col_ref[a, 2 * g + m]
                    for b in range(8):
                        at = pl.ds(row_ref[a, b] * (8 * B) + slot, B, stride=8)
                        out_ref[at, :] = out_ref[at, :] - prod[b * B : (b + 1) * B, m * B : (m + 1) * B]

            return carry

        lax.fori_loop(0, (count + 1) // 2, pair, 0)


def extend(counts, col_slots, row_slots, front, r0, r1, c0, c1):
    smem = pl.BlockSpec(memory_space=pltpu.SMEM)
    vmem = pl.BlockSpec(memory_space=pltpu.VMEM)
    return pl.pallas_call(
        extend_kernel,
        out_shape=jax.ShapeDtypeStruct(front.shape, F32),
        in_specs=[smem] * 3 + [vmem] * 5,
        out_specs=vmem,
        scratch_shapes=[pltpu.VMEM((8 * B, 2 * B), F32)],
        compiler_params=pltpu.CompilerParams(vmem_limit_bytes=VMEM_BYTES),
        name="extend_add",
    )(counts, col_slots, row_slots, front, r0, r1, c0, c1)


def move(x, target):
    def flat(c):
        return int(np.ravel_multi_index(c, SIZES))

    pairs = [(flat(c), flat(target(*c))) for c in np.ndindex(*SIZES)]
    return lax.ppermute(x, AXES, pairs)


def step_z(by):
    return lambda yhi, x, ylo, z, core: (yhi, x, ylo, (z + by) % 4, core)


def step_x(by):
    return lambda yhi, x, ylo, z, core: (yhi, (x + by) % 4, ylo, z, core)


def step_y(by):
    def target(yhi, x, ylo, z, core):
        y = (yhi * 2 + ylo + by) % 4
        return (y // 2, x, y % 2, z, core)

    return target


def step_first(by):
    return lambda *c: (step_x(by) if c[4] == 0 else step_y(by))(*c)


def step_second(by):
    return lambda *c: (step_y(by) if c[4] == 0 else step_x(by))(*c)


def ring(x, step):
    return x, move(x, step(1)), move(x, step(2)), move(x, step(-1))


def after(x, done):
    return lax.optimization_barrier((x, done))


def axis_groups(stage):
    groups = {}
    for c in np.ndindex(*SIZES):
        yhi, x, ylo, z, core = c
        along_x = core == stage
        key = (core, z, yhi, ylo) if along_x else (core, z, x)
        groups.setdefault(key, []).append((x if along_x else yhi * 2 + ylo, int(np.ravel_multi_index(c, SIZES))))
    return [[device for _, device in sorted(group)] for group in groups.values()]


def swap(x):
    return move(x, lambda yhi, x, ylo, z, core: (yhi, x, ylo, z, 1 - core))


def to_col_group(yhi, x, ylo, z, core):
    shift = z if core == 0 else (z + 2) % 4
    y = (yhi * 2 + ylo + shift) % 4
    return (y // 2, x if core == 0 else 3 - x, y % 2, yhi * 2 + x // 2, ylo)


def pick(x, index):
    return lax.dynamic_index_in_dim(x, index, 0, keepdims=False)


def per_device(child_pivot, child_panel, child_map, panel_mask, parent_front):
    yhi, x, ylo, z, core = (lax.axis_index(name) for name in AXES)
    row = yhi * 4 + x
    y = yhi * 2 + ylo
    at = jnp.stack([yhi, x, ylo, z, core]).astype(jnp.int32)
    n = child_pivot.shape[2]
    np_ = n // PW

    other = swap(pick(child_pivot, 1 - core))
    own = pick(child_pivot, core)
    strip = jnp.where(core == 0, jnp.concatenate([own, other]), jnp.concatenate([other, own]))
    strip = strip.reshape(STRIP, np_, PW).transpose(1, 0, 2)

    def plane(part):
        part = jnp.stack(ring(part, step_z), axis=1)
        return jnp.stack(ring(part, step_first), axis=1).reshape(2, 16 * STRIP, PW)

    mask = pick(pick(panel_mask, ylo), row * 8 + z * 2 + core)
    kept = (child_panel.reshape(B, n // B, B) * mask.astype(BF16)[None, :, None]).reshape(B, n)
    first = plane(strip[:2])
    first, kept = after(first, kept)
    for_col = move(kept, to_col_group)
    back, ahead = move(first, step_second(1)), move(first, step_second(-1))
    far = move(back[:1], step_second(1)), move(ahead[1:], step_second(-1))
    rest = plane(after(strip[2:], first)[0])

    maps = child_map.reshape(2, 8, 8)
    maps = jnp.stack([pick(maps, core), pick(maps, 1 - core)])
    slots = maps // 8
    row_slots = lax.dynamic_index_in_dim(slots, row, 1, keepdims=False)
    by_col = lax.dynamic_slice_in_dim(slots, 2 * z, 2, axis=1)
    needed = by_col % 2 == ylo
    place = jnp.cumsum(needed.astype(jnp.int32), axis=2) - 1
    hit = (place[..., None, :] == jnp.arange(8)[:, None]) & needed[..., None, :]
    i = jnp.arange(8)
    from_z, from_core = (i // 2)[None, :], (i % 2)[None, :]
    from_x = 2 * (z % 2) + jnp.arange(2)[:, None]
    x_of = jnp.where(from_core == 0, from_x, 3 - from_x)
    y_of = (2 * (z // 2) + core + from_z + 2 * from_core) % 4 + 0 * x_of
    where = jnp.where(core == 0, y_of * 4 + x_of, x_of * 4 + y_of)
    order = jnp.sum(jnp.where(hit[0], where[:, None, :], 0), axis=2).astype(jnp.int32)
    col_slots = jnp.sum(jnp.where(hit, (by_col // 2)[..., None, :], 0), axis=3).astype(jnp.int32)
    counts = jnp.sum(needed, axis=2).astype(jnp.int32)

    mine_cols = lax.dynamic_index_in_dim(col_slots, core, 1, keepdims=False)
    mine_counts = lax.dynamic_index_in_dim(counts, core, 1, keepdims=False)
    ask_near = (pick(counts[0], 1 - core)[None], pick(order, 1 - core))
    ask_own = (pick(counts[0], core)[None], pick(order, core))
    small = (mine_cols, mine_counts, row_slots, ask_near, ask_own)

    (small, rest, for_col), arrived = after((small, rest, for_col), (back, ahead) + far)
    mine_cols, mine_counts, row_slots, ask_near, ask_own = small
    back, ahead, *far = arrived
    near_rest = move(rest, step_second(1)), move(rest, step_second(-1))
    for_col = lax.all_gather(for_col, AXES, axis=0, axis_index_groups=axis_groups(0))

    panels = [factor_panel(0, n, at, [(first, 0), (back, 0), (far[0], 0), (ahead, 0)], [])]
    (near_rest, for_col), panels[0] = after((near_rest, for_col), panels[0])
    back2, ahead2 = near_rest
    far2 = move(back2[:1], step_second(1)), move(ahead2[1:], step_second(-1))
    for_col = lax.all_gather(for_col, AXES, axis=0, axis_index_groups=axis_groups(1))
    panels.append(factor_panel(1, n, at, [(first, 1), (back, 1), (far[1], 0), (ahead, 1)], panels))
    (far2, kept), panels[1] = after((far2, kept), panels[1])
    row_panel = lax.all_gather(kept, ("ylo", "z", "core"), axis=0)
    for s in range(2, np_):
        panels.append(factor_panel(s, n, at, [(rest, s - 2), (back2, s - 2), (far2[s - 2], 0), (ahead2, s - 2)], panels))
    col_panel = for_col.reshape(16, B, n)

    col_other = swap(solve(col_panel, *ask_near, panels))
    row_order = core * 8 + jnp.arange(8, dtype=jnp.int32)
    row_side = solve(row_panel, jnp.full((1,), 8, jnp.int32), row_order, panels)
    row_other = swap(row_side)
    row_side, col_panel = after(row_side, col_panel)
    col_own = solve(col_panel, *ask_own, panels)

    front = parent_front.reshape(-1, B)
    out = extend(mine_counts, mine_cols, row_slots, front, row_side, row_other, col_own, col_other)
    return out.reshape(parent_front.shape)


def solution(mesh):
    rows, cols = AXES[:2], AXES[2:]
    split_mesh = Mesh(mesh.devices.reshape(SIZES), AXES)
    front = P(None, rows, None, None, cols, None)
    return jax.shard_map(
        per_device,
        mesh=split_mesh,
        in_specs=(P(None, AXES, None), P(rows, cols, None, None), P(), P(), front),
        out_specs=front,
        check_vma=False,
    )
```

```python
import functools

import jax
import jax.numpy as jnp
import numpy as np
from jax import lax
from jax.experimental import pallas as pl
from jax.experimental.pallas import tpu as pltpu
from jax.sharding import Mesh, PartitionSpec as P

F32 = jnp.float32
BF16 = jnp.bfloat16
B = 128
PW = 512
VMEM_BYTES = 28 << 20
STRIP = 32
AXES = ("yhi", "x", "ylo", "z", "core")
SIZES = (2, 4, 2, 4, 2)


def split(x):
    hi = x.astype(BF16)
    return hi, (x - hi.astype(F32)).astype(BF16)


def dot_t(x, y):
    return lax.dot_general(x, y, (((1,), (1,)), ((), ())), preferred_element_type=F32)


def dot3_t(xh, xl, yh, yl):
    return dot_t(jnp.concatenate([xh, xh, xl], axis=1), jnp.concatenate([yh, yl, yh], axis=1))


def leaf_inverse(block):
    lane = lax.broadcasted_iota(jnp.int32, (8, B), 1)
    sub = lax.broadcasted_iota(jnp.int32, (8, B), 0)
    groups = B // 8
    rows = [block[8 * i : 8 * i + 8, :] for i in range(groups)]

    def row_of(x, j):
        return jnp.broadcast_to(x[j : j + 1, :], (8, B))

    def col_of(x, j):
        return jnp.broadcast_to(x[:, j : j + 1], (8, B))

    def total(p):
        return ((p[0] + p[1]) + (p[2] + p[3])) + ((p[4] + p[5]) + (p[6] + p[7]))

    done = []
    cols = [col_of(rows[0], j) for j in range(8)]
    for t in range(groups):
        lo = 8 * t
        rel = lane - lo
        inside = (rel >= 0) & (rel < 8)
        last = t == groups - 1
        if not last:
            ahead = [col_of(rows[t], lo + 8 + j) for j in range(8)]
            below = [col_of(rows[t + 1], lo + 8 + j) for j in range(8)]
            left = [col_of(rows[t + 1], lo + j) for j in range(8)]
        half = jnp.where(inside, jnp.where(rel == sub, 1.0, 0.0), rows[t])
        full = half
        pivots = jnp.ones((8, B), F32)
        recips = jnp.ones((8, B), F32)
        for j in range(8):
            pivot = row_of(cols[j], j)
            recip = pltpu.reciprocal(pivot, approx=True)
            pivots = jnp.where(sub == j, pivot, pivots)
            recips = jnp.where(sub == j, recip, recips)
            mult = jnp.where(sub != j, cols[j], 0.0) * recip
            for jj in range(j + 1, 8):
                cols[jj] = cols[jj] - mult * row_of(cols[jj], j)
            row = row_of(half, j)
            half = half - jnp.where(sub > j, mult, 0.0) * row
            full = full - mult * row
            if not last:
                ahead = [c - mult * row_of(c, j) for c in ahead]
        full = full * recips
        done.append(jnp.where(lane <= sub + lo, half * lax.rsqrt(pivots), 0.0))
        if last:
            break
        ahead = [c * recips for c in ahead]
        cols = [b - total([left[j] * row_of(c, j) for j in range(8)]) for b, c in zip(below, ahead)]
        rows[t + 1] = jnp.where(inside, 0.0, rows[t + 1]) - total([left[j] * row_of(full, j) for j in range(8)])
        if t + 2 < groups:
            lh, ll = split(jnp.concatenate([jnp.where(inside, r, 0.0) for r in rows[t + 2 :]], axis=0))
            zero = jnp.zeros((8, B), F32)
            fh, fl = split(jnp.concatenate([full if i == t else zero for i in range(groups)], axis=0))
            less = jnp.dot(
                jnp.concatenate([lh, lh, ll], axis=1),
                jnp.concatenate([fh, fl, fh], axis=0),
                preferred_element_type=F32,
            )
            for i in range(t + 2, groups):
                rows[i] = jnp.where(inside, 0.0, rows[i]) - less[8 * (i - t - 2) : 8 * (i - t - 1)]
    return jnp.concatenate(done, axis=0)


def place_strips(s, at_ref, pieces, work):
    yhi, x, ylo, z, core = (at_ref[i] for i in range(5))
    y = yhi * 2 + ylo
    for far, ref in enumerate(pieces):

        def strip(g, carry, ref=ref, far=far):
            mid, near = g // 4, g % 4
            xx = (x - jnp.where(core == 0, mid, far)) & 3
            yy = (y - jnp.where(core == 0, far, mid)) & 3
            zz = (z - near) & 3
            row = ((yy // 2) * 4 + xx) * 8 + (yy % 2) * 4 + zz
            rows = pl.ds(pl.multiple_of(g * STRIP, STRIP), STRIP)
            to = pl.ds(pl.multiple_of(row * STRIP, STRIP), STRIP)

            @pl.when(row >= s * PW // STRIP)
            def _():
                work[to, :] = ref[0, rows, :].astype(F32)

            return carry

        lax.fori_loop(0, ref.shape[1] // STRIP, strip, 0)


def panel_kernel(s, at_ref, *refs):
    pieces, refs = refs[:4], refs[4:]
    prev = [(refs[2 * p], refs[2 * p + 1]) for p in range(s)]
    hi_ref, lo_ref, work, square = refs[2 * s :]
    n = work.shape[0]
    base = s * PW
    place_strips(s, at_ref, pieces, work)

    def load(pair, rows):
        return pair[0][rows, :], pair[1][rows, :]

    right = [load(pair, pl.ds(base, PW)) for pair in prev]

    def left(rows, p):
        return dot3_t(*load(prev[p], rows), *right[p])

    def own_rows(c, carry):
        rows = pl.ds(pl.multiple_of(base + c * 256, 256), 256)
        total = work[rows, :]
        for p in range(s):
            total = total - left(rows, p)
        square[pl.ds(pl.multiple_of(c * 256, 256), 256), :] = total
        return carry

    lax.fori_loop(0, PW // 256, own_rows, 0)

    def other_rows(k):
        if s == 0:
            return
        count = (n - PW) // (4 * B)
        at = [k * ((n - PW) // 4) + i * B for i in range(count)]
        at = [jnp.where(row < base, row, row + PW) for row in at]
        rows = [pl.ds(pl.multiple_of(row, B), B) for row in at]
        total = jnp.concatenate([jnp.where(row > base, work[r, :], 0.0) for row, r in zip(at, rows)], axis=0)
        for p in range(s):
            part = [load(prev[p], r) for r in rows]
            product = dot3_t(*[jnp.concatenate(half, axis=0) for half in zip(*part)], *right[p])
            use = [(row > base) | (row < (p + 1) * PW) for row in at]
            use = [jnp.broadcast_to(u.astype(F32), (B, PW)) for u in use]
            total = total - product * jnp.concatenate(use, axis=0)
        for i, r in enumerate(rows):
            work[r, :] = total[i * B : (i + 1) * B]

    eye = (lax.broadcasted_iota(jnp.int32, (B, B), 0) == lax.broadcasted_iota(jnp.int32, (B, B), 1)).astype(F32)

    def step(k, carry):
        cols = pl.ds(pl.multiple_of(k * B, B), B)
        block = square[cols, cols]
        other_rows(k)
        inv = leaf_inverse(block)
        square[cols, cols] = eye
        qh, ql = split(dot3_t(*split(square[:, cols]), *split(inv)))
        hi_ref[pl.ds(base, PW), cols] = qh
        lo_ref[pl.ds(base, PW), cols] = ql
        for kk in range(PW // B - 1):

            @pl.when(k == kk)
            def _(kk=kk):
                width = PW - (kk + 1) * B
                at = pl.ds(kk * B, B)
                later = pl.ds((kk + 1) * B, width)
                below = pl.ds(base + (kk + 1) * B, width)
                square[at, later] = jnp.zeros((B, width), F32)
                yh, yl = hi_ref[below, at], lo_ref[below, at]
                qh, ql = hi_ref[pl.ds(base, PW), at], lo_ref[pl.ds(base, PW), at]
                square[:, later] = square[:, later] - dot3_t(qh, ql, yh, yl)
                hi_ref[below, at] = jnp.zeros((width, B), BF16)
                lo_ref[below, at] = jnp.zeros((width, B), BF16)

        return carry

    lax.fori_loop(0, PW // B, step, 0)
    vh, vl = hi_ref[pl.ds(base, PW), :], lo_ref[pl.ds(base, PW), :]
    stacked = jnp.concatenate([vh, vl, vh], axis=0)
    for rb in range(n // PW):
        if rb != s:

            def rest(c, carry, rb=rb):
                rows = pl.ds(pl.multiple_of(rb * PW + c * 256, 256), 256)
                xh, xl = split(work[rows, :])
                q = jnp.dot(jnp.concatenate([xh, xh, xl], axis=1), stacked, preferred_element_type=F32)
                hi_ref[rows, :], lo_ref[rows, :] = split(q)
                return carry

            lax.fori_loop(0, PW // 256, rest, 0)


def factor_panel(s, n, at, pieces, prev):
    flat = [x for pair in prev for x in pair]
    full = pl.BlockSpec(memory_space=pltpu.VMEM)
    out = jax.ShapeDtypeStruct((n, PW), BF16)
    return pl.pallas_call(
        functools.partial(panel_kernel, s),
        grid=(1,),
        out_shape=(out, out),
        in_specs=[pl.BlockSpec(memory_space=pltpu.SMEM)]
        + [
            pl.BlockSpec((1,) + x.shape[1:], lambda g, i=i: (i, 0, 0), pipeline_mode=pl.Buffered(1)) for x, i in pieces
        ]
        + [full] * len(flat),
        out_specs=(full, full),
        scratch_shapes=[pltpu.VMEM((n, PW), F32), pltpu.VMEM((PW, PW), F32)],
        compiler_params=pltpu.CompilerParams(vmem_limit_bytes=VMEM_BYTES),
        cost_estimate=pl.CostEstimate(flops=30 * 10**9, bytes_accessed=10**7, transcendentals=0),
        name="factor_panel",
    )(at, *[x for x, _ in pieces], *flat)


def times_inverse(x, v_refs, store):
    for s in range(len(v_refs) // 2):
        vh, vl = v_refs[2 * s], v_refs[2 * s + 1]
        part = x[:, : (s + 1) * PW]
        both = jnp.concatenate([part, part], axis=1)
        v = jnp.concatenate([vh[...], vl[...]], axis=0)
        store(s, jnp.dot(both, v, preferred_element_type=F32).astype(BF16))


def v_specs(count):
    specs = []
    for s in range(count):
        spec = pl.BlockSpec(((s + 1) * PW, PW), lambda *_: (0, 0), pipeline_mode=pl.Buffered(1))
        specs += [spec, spec]
    return specs


def solve_kernel(count_ref, order_ref, x0_ref, x1_ref, *refs):
    out_ref = refs[-1]

    @pl.when(2 * pl.program_id(0) < count_ref[0])
    def _():
        def store(s, value):
            out_ref[:, s * PW : (s + 1) * PW] = value

        times_inverse(jnp.concatenate([x0_ref[0], x1_ref[0]], axis=0), refs[:-1], store)


def solve(x, count, order, panels):
    n = x.shape[2]
    flat = [v for pair in panels for v in pair]
    return pl.pallas_call(
        solve_kernel,
        grid_spec=pltpu.PrefetchScalarGridSpec(
            num_scalar_prefetch=2,
            grid=(4,),
            in_specs=[
                pl.BlockSpec((1, B, n), lambda g, c, o: (o[2 * g], 0, 0)),
                pl.BlockSpec((1, B, n), lambda g, c, o: (o[2 * g + 1], 0, 0)),
            ]
            + v_specs(len(panels)),
            out_specs=pl.BlockSpec((2 * B, n), lambda g, c, o: (g, 0)),
        ),
        out_shape=jax.ShapeDtypeStruct((8 * B, n), BF16),
        compiler_params=pltpu.CompilerParams(vmem_limit_bytes=VMEM_BYTES),
        cost_estimate=pl.CostEstimate(flops=12 * 10**9, bytes_accessed=2 * 10**7, transcendentals=0),
        name="solve",
    )(count, order, x, x, *flat)


def extend_kernel(count_ref, col_ref, row_ref, front_ref, r0_ref, r1_ref, c0_ref, c1_ref, out_ref, prod):
    total = front_ref.shape[0]

    def fill(c, carry):
        rows = pl.ds(pl.multiple_of(c * 1024, 1024), 1024)
        out_ref[rows, :] = front_ref[rows, :].astype(F32)
        return carry

    lax.fori_loop(0, total // 1024, fill, 0)
    for a, (r_ref, c_ref) in enumerate(((r0_ref, c0_ref), (r1_ref, c1_ref))):
        count = count_ref[a]

        def pair(g, carry, a=a, r_ref=r_ref, c_ref=c_ref, count=count):
            right = c_ref[pl.ds(pl.multiple_of(g * 2 * B, 2 * B), 2 * B), :]

            def half(h, inner):
                rows = pl.ds(pl.multiple_of(h * 512, 512), 512)
                prod[rows, :] = dot_t(r_ref[rows, :], right)
                return inner

            lax.fori_loop(0, 2, half, 0)
            for m in range(2):

                @pl.when(2 * g + m < count)
                def _(m=m):
                    slot = col_ref[a, 2 * g + m]
                    for b in range(8):
                        at = pl.ds(row_ref[a, b] * (8 * B) + slot, B, stride=8)
                        out_ref[at, :] = out_ref[at, :] - prod[b * B : (b + 1) * B, m * B : (m + 1) * B]

            return carry

        lax.fori_loop(0, (count + 1) // 2, pair, 0)


def extend(counts, col_slots, row_slots, front, r0, r1, c0, c1):
    smem = pl.BlockSpec(memory_space=pltpu.SMEM)
    vmem = pl.BlockSpec(memory_space=pltpu.VMEM)
    return pl.pallas_call(
        extend_kernel,
        out_shape=jax.ShapeDtypeStruct(front.shape, F32),
        in_specs=[smem] * 3 + [vmem] * 5,
        out_specs=vmem,
        scratch_shapes=[pltpu.VMEM((8 * B, 2 * B), F32)],
        compiler_params=pltpu.CompilerParams(vmem_limit_bytes=32 << 20),
        name="extend_add",
    )(counts, col_slots, row_slots, front, r0, r1, c0, c1)


def move(x, target):
    def flat(c):
        return int(np.ravel_multi_index(c, SIZES))

    pairs = [(flat(c), flat(target(*c))) for c in np.ndindex(*SIZES)]
    return lax.ppermute(x, AXES, pairs)


def step_z(by):
    return lambda yhi, x, ylo, z, core: (yhi, x, ylo, (z + by) % 4, core)


def step_x(by):
    return lambda yhi, x, ylo, z, core: (yhi, (x + by) % 4, ylo, z, core)


def step_y(by):
    def target(yhi, x, ylo, z, core):
        y = (yhi * 2 + ylo + by) % 4
        return (y // 2, x, y % 2, z, core)

    return target


def step_first(by):
    return lambda *c: (step_x(by) if c[4] == 0 else step_y(by))(*c)


def step_second(by):
    return lambda *c: (step_y(by) if c[4] == 0 else step_x(by))(*c)


def ring(x, step):
    return x, move(x, step(1)), move(x, step(2)), move(x, step(-1))


def after(x, done):
    return lax.optimization_barrier((x, done))


def axis_groups(stage):
    groups = {}
    for c in np.ndindex(*SIZES):
        yhi, x, ylo, z, core = c
        along_x = core == stage
        key = (core, z, yhi, ylo) if along_x else (core, z, x)
        groups.setdefault(key, []).append((x if along_x else yhi * 2 + ylo, int(np.ravel_multi_index(c, SIZES))))
    return [[device for _, device in sorted(group)] for group in groups.values()]


def swap(x):
    return move(x, lambda yhi, x, ylo, z, core: (yhi, x, ylo, z, 1 - core))


def to_col_group(yhi, x, ylo, z, core):
    shift = z if core == 0 else (z + 2) % 4
    y = (yhi * 2 + ylo + shift) % 4
    return (y // 2, x if core == 0 else 3 - x, y % 2, yhi * 2 + x // 2, ylo)


def pick(x, index):
    return lax.dynamic_index_in_dim(x, index, 0, keepdims=False)


def per_device(child_pivot, child_panel, child_map, panel_mask, parent_front):
    yhi, x, ylo, z, core = (lax.axis_index(name) for name in AXES)
    row = yhi * 4 + x
    y = yhi * 2 + ylo
    at = jnp.stack([yhi, x, ylo, z, core]).astype(jnp.int32)
    n = child_pivot.shape[2]
    np_ = n // PW

    other = swap(pick(child_pivot, 1 - core))
    own = pick(child_pivot, core)
    strip = jnp.where(core == 0, jnp.concatenate([own, other]), jnp.concatenate([other, own]))
    strip = strip.reshape(STRIP, np_, PW).transpose(1, 0, 2)

    mask = pick(pick(panel_mask, ylo), row * 8 + z * 2 + core)
    kept = (child_panel.reshape(B, n // B, B) * mask.astype(BF16)[None, :, None]).reshape(B, n)
    near = jnp.stack(ring(strip, step_z), axis=1)
    parts = ring(near, step_first)
    first = jnp.stack([part[:2] for part in parts], axis=1).reshape(2, 16 * STRIP, PW)
    first, kept = after(first, kept)
    for_col = move(kept, to_col_group)
    back, ahead = move(first, step_second(1)), move(first, step_second(-1))
    far = move(back[:1], step_second(1)), move(ahead[1:], step_second(-1))
    parts, first = after(parts, first)
    rest = jnp.stack([part[2:] for part in parts], axis=1).reshape(2, 16 * STRIP, PW)

    maps = child_map.reshape(2, 8, 8)
    maps = jnp.stack([pick(maps, core), pick(maps, 1 - core)])
    slots = maps // 8
    row_slots = lax.dynamic_index_in_dim(slots, row, 1, keepdims=False)
    by_col = lax.dynamic_slice_in_dim(slots, 2 * z, 2, axis=1)
    needed = by_col % 2 == ylo
    place = jnp.cumsum(needed.astype(jnp.int32), axis=2) - 1
    hit = (place[..., None, :] == jnp.arange(8)[:, None]) & needed[..., None, :]
    i = jnp.arange(8)
    from_z, from_core = (i // 2)[None, :], (i % 2)[None, :]
    from_x = 2 * (z % 2) + jnp.arange(2)[:, None]
    x_of = jnp.where(from_core == 0, from_x, 3 - from_x)
    y_of = (2 * (z // 2) + core + from_z + 2 * from_core) % 4 + 0 * x_of
    where = jnp.where(core == 0, y_of * 4 + x_of, x_of * 4 + y_of)
    order = jnp.sum(jnp.where(hit[0], where[:, None, :], 0), axis=2).astype(jnp.int32)
    col_slots = jnp.sum(jnp.where(hit, (by_col // 2)[..., None, :], 0), axis=3).astype(jnp.int32)
    counts = jnp.sum(needed, axis=2).astype(jnp.int32)

    mine_cols = lax.dynamic_index_in_dim(col_slots, core, 1, keepdims=False)
    mine_counts = lax.dynamic_index_in_dim(counts, core, 1, keepdims=False)
    ask_near = (pick(counts[0], 1 - core)[None], pick(order, 1 - core))
    ask_own = (pick(counts[0], core)[None], pick(order, core))
    small = (mine_cols, mine_counts, row_slots, ask_near, ask_own)

    (small, rest, for_col), arrived = after((small, rest, for_col), (back, ahead) + far)
    mine_cols, mine_counts, row_slots, ask_near, ask_own = small
    back, ahead, *far = arrived
    near_rest = move(rest, step_second(1)), move(rest, step_second(-1))
    for_col = lax.all_gather(for_col, AXES, axis=0, axis_index_groups=axis_groups(0))

    panels = [factor_panel(0, n, at, [(first, 0), (back, 0), (far[0], 0), (ahead, 0)], [])]
    (near_rest, for_col), panels[0] = after((near_rest, for_col), panels[0])
    back2, ahead2 = near_rest
    far2 = move(back2[:1], step_second(1)), move(ahead2[1:], step_second(-1))
    for_col = lax.all_gather(for_col, AXES, axis=0, axis_index_groups=axis_groups(1))
    panels.append(factor_panel(1, n, at, [(first, 1), (back, 1), (far[1], 0), (ahead, 1)], panels))
    (far2, kept), panels[1] = after((far2, kept), panels[1])
    row_panel = lax.all_gather(kept, ("ylo", "z", "core"), axis=0)
    for s in range(2, np_):
        panels.append(factor_panel(s, n, at, [(rest, s - 2), (back2, s - 2), (far2[s - 2], 0), (ahead2, s - 2)], panels))
    col_panel = for_col.reshape(16, B, n)

    col_other = swap(solve(col_panel, *ask_near, panels))
    row_order = core * 8 + jnp.arange(8, dtype=jnp.int32)
    row_side = solve(row_panel, jnp.full((1,), 8, jnp.int32), row_order, panels)
    row_other = swap(row_side)
    row_side, col_panel = after(row_side, col_panel)
    col_own = solve(col_panel, *ask_own, panels)

    front = parent_front.reshape(-1, B)
    out = extend(mine_counts, mine_cols, row_slots, front, row_side, row_other, col_own, col_other)
    return out.reshape(parent_front.shape)


def solution(mesh):
    rows, cols = AXES[:2], AXES[2:]
    split_mesh = Mesh(mesh.devices.reshape(SIZES), AXES)
    front = P(None, rows, None, None, cols, None)
    return jax.shard_map(
        per_device,
        mesh=split_mesh,
        in_specs=(P(None, AXES, None), P(rows, cols, None, None), P(), P(), front),
        out_specs=front,
        check_vma=False,
    )
```

```python
import functools

import jax
import jax.numpy as jnp
import numpy as np
from jax import lax
from jax.experimental import pallas as pl
from jax.experimental.pallas import tpu as pltpu
from jax.sharding import Mesh, PartitionSpec as P

F32 = jnp.float32
BF16 = jnp.bfloat16
B = 128
PW = 512
VMEM_BYTES = 56 << 20
STRIP = 32
AXES = ("yhi", "x", "ylo", "z", "core")
SIZES = (2, 4, 2, 4, 2)


def split(x):
    hi = x.astype(BF16)
    return hi, (x - hi.astype(F32)).astype(BF16)


def dot_t(x, y):
    return lax.dot_general(x, y, (((1,), (1,)), ((), ())), preferred_element_type=F32)


def dot3_t(xh, xl, yh, yl):
    return dot_t(jnp.concatenate([xh, xh, xl], axis=1), jnp.concatenate([yh, yl, yh], axis=1))


def leaf_inverse(block):
    lane = lax.broadcasted_iota(jnp.int32, (8, B), 1)
    sub = lax.broadcasted_iota(jnp.int32, (8, B), 0)
    groups = B // 8
    rows = [block[8 * i : 8 * i + 8, :] for i in range(groups)]

    def row_of(x, j):
        return jnp.broadcast_to(x[j : j + 1, :], (8, B))

    def col_of(x, j):
        return jnp.broadcast_to(x[:, j : j + 1], (8, B))

    def total(p):
        return ((p[0] + p[1]) + (p[2] + p[3])) + ((p[4] + p[5]) + (p[6] + p[7]))

    done = []
    cols = [col_of(rows[0], j) for j in range(8)]
    for t in range(groups):
        lo = 8 * t
        rel = lane - lo
        inside = (rel >= 0) & (rel < 8)
        last = t == groups - 1
        if not last:
            ahead = [col_of(rows[t], lo + 8 + j) for j in range(8)]
            below = [col_of(rows[t + 1], lo + 8 + j) for j in range(8)]
            left = [col_of(rows[t + 1], lo + j) for j in range(8)]
        half = jnp.where(inside, jnp.where(rel == sub, 1.0, 0.0), rows[t])
        full = half
        pivots = jnp.ones((8, B), F32)
        recips = jnp.ones((8, B), F32)
        for j in range(8):
            pivot = row_of(cols[j], j)
            recip = pltpu.reciprocal(pivot, approx=True)
            pivots = jnp.where(sub == j, pivot, pivots)
            recips = jnp.where(sub == j, recip, recips)
            mult = jnp.where(sub != j, cols[j], 0.0) * recip
            for jj in range(j + 1, 8):
                cols[jj] = cols[jj] - mult * row_of(cols[jj], j)
            row = row_of(half, j)
            half = half - jnp.where(sub > j, mult, 0.0) * row
            full = full - mult * row
            if not last:
                ahead = [c - mult * row_of(c, j) for c in ahead]
        full = full * recips
        done.append(jnp.where(lane <= sub + lo, half * lax.rsqrt(pivots), 0.0))
        if last:
            break
        ahead = [c * recips for c in ahead]
        cols = [b - total([left[j] * row_of(c, j) for j in range(8)]) for b, c in zip(below, ahead)]
        rows[t + 1] = jnp.where(inside, 0.0, rows[t + 1]) - total([left[j] * row_of(full, j) for j in range(8)])
        if t + 2 < groups:
            lh, ll = split(jnp.concatenate([jnp.where(inside, r, 0.0) for r in rows[t + 2 :]], axis=0))
            zero = jnp.zeros((8, B), F32)
            fh, fl = split(jnp.concatenate([full if i == t else zero for i in range(groups)], axis=0))
            less = jnp.dot(
                jnp.concatenate([lh, lh, ll], axis=1),
                jnp.concatenate([fh, fl, fh], axis=0),
                preferred_element_type=F32,
            )
            for i in range(t + 2, groups):
                rows[i] = jnp.where(inside, 0.0, rows[i]) - less[8 * (i - t - 2) : 8 * (i - t - 1)]
    return jnp.concatenate(done, axis=0)


def place_strips(s, at_ref, pieces, work):
    yhi, x, ylo, z, core = (at_ref[i] for i in range(5))
    y = yhi * 2 + ylo
    for far, ref in enumerate(pieces):

        def strip(g, carry, ref=ref, far=far):
            mid, near = g // 4, g % 4
            xx = (x - jnp.where(core == 0, mid, far)) & 3
            yy = (y - jnp.where(core == 0, far, mid)) & 3
            zz = (z - near) & 3
            row = ((yy // 2) * 4 + xx) * 8 + (yy % 2) * 4 + zz
            rows = pl.ds(pl.multiple_of(g * STRIP, STRIP), STRIP)
            to = pl.ds(pl.multiple_of(row * STRIP, STRIP), STRIP)

            @pl.when(row >= s * PW // STRIP)
            def _():
                work[to, :] = ref[0, rows, :].astype(F32)

            return carry

        lax.fori_loop(0, ref.shape[1] // STRIP, strip, 0)


def panel_kernel(s, count, at_ref, *refs):
    pieces, refs = refs[: 4 * count], refs[4 * count :]
    prev = [(refs[2 * p], refs[2 * p + 1]) for p in range(s + count)]
    work, square = refs[2 * (s + count) :]
    for i in range(count):
        one_panel(s + i, at_ref, pieces[4 * i : 4 * i + 4], prev[: s + i], *prev[s + i], work, square)


def one_panel(s, at_ref, pieces, prev, hi_ref, lo_ref, work, square):
    n = work.shape[0]
    base = s * PW
    place_strips(s, at_ref, pieces, work)

    def load(pair, rows):
        return pair[0][rows, :], pair[1][rows, :]

    right = [load(pair, pl.ds(base, PW)) for pair in prev]

    def left(rows, p):
        return dot3_t(*load(prev[p], rows), *right[p])

    def own_rows(c, carry):
        rows = pl.ds(pl.multiple_of(base + c * 256, 256), 256)
        total = work[rows, :]
        for p in range(s):
            total = total - left(rows, p)
        square[pl.ds(pl.multiple_of(c * 256, 256), 256), :] = total
        return carry

    lax.fori_loop(0, PW // 256, own_rows, 0)

    def other_rows(k):
        if s == 0:
            return
        count = (n - PW) // (4 * B)
        at = [k * ((n - PW) // 4) + i * B for i in range(count)]
        at = [jnp.where(row < base, row, row + PW) for row in at]
        rows = [pl.ds(pl.multiple_of(row, B), B) for row in at]
        total = jnp.concatenate([jnp.where(row > base, work[r, :], 0.0) for row, r in zip(at, rows)], axis=0)
        for p in range(s):
            part = [load(prev[p], r) for r in rows]
            product = dot3_t(*[jnp.concatenate(half, axis=0) for half in zip(*part)], *right[p])
            use = [(row > base) | (row < (p + 1) * PW) for row in at]
            use = [jnp.broadcast_to(u.astype(F32), (B, PW)) for u in use]
            total = total - product * jnp.concatenate(use, axis=0)
        for i, r in enumerate(rows):
            work[r, :] = total[i * B : (i + 1) * B]

    eye = (lax.broadcasted_iota(jnp.int32, (B, B), 0) == lax.broadcasted_iota(jnp.int32, (B, B), 1)).astype(F32)

    def step(k, carry):
        cols = pl.ds(pl.multiple_of(k * B, B), B)
        block = square[cols, cols]
        other_rows(k)
        inv = leaf_inverse(block)
        square[cols, cols] = eye
        qh, ql = split(dot3_t(*split(square[:, cols]), *split(inv)))
        hi_ref[pl.ds(base, PW), cols] = qh
        lo_ref[pl.ds(base, PW), cols] = ql
        for kk in range(PW // B - 1):

            @pl.when(k == kk)
            def _(kk=kk):
                width = PW - (kk + 1) * B
                at = pl.ds(kk * B, B)
                later = pl.ds((kk + 1) * B, width)
                below = pl.ds(base + (kk + 1) * B, width)
                square[at, later] = jnp.zeros((B, width), F32)
                yh, yl = hi_ref[below, at], lo_ref[below, at]
                qh, ql = hi_ref[pl.ds(base, PW), at], lo_ref[pl.ds(base, PW), at]
                square[:, later] = square[:, later] - dot3_t(qh, ql, yh, yl)
                hi_ref[below, at] = jnp.zeros((width, B), BF16)
                lo_ref[below, at] = jnp.zeros((width, B), BF16)

        return carry

    lax.fori_loop(0, PW // B, step, 0)
    half = PW // 2
    parts = []
    for h in range(2):
        at = pl.ds(base, (h + 1) * half), pl.ds(h * half, half)
        vh, vl = hi_ref[at], lo_ref[at]
        parts.append(jnp.concatenate([vh, vl, vh], axis=0))
    for rb in range(n // PW):
        if rb != s:

            def rest(c, carry, rb=rb):
                rows = pl.ds(pl.multiple_of(rb * PW + c * 256, 256), 256)
                xh, xl = split(work[rows, :])
                for h in range(2):
                    ah, al = xh[:, : (h + 1) * half], xl[:, : (h + 1) * half]
                    q = jnp.dot(jnp.concatenate([ah, ah, al], axis=1), parts[h], preferred_element_type=F32)
                    cols = pl.ds(h * half, half)
                    hi_ref[rows, cols], lo_ref[rows, cols] = split(q)
                return carry

            lax.fori_loop(0, PW // 256, rest, 0)


def factor_panels(s, n, at, pieces, prev):
    count = len(pieces) // 4
    flat = [x for pair in prev for x in pair]
    full = pl.BlockSpec(memory_space=pltpu.VMEM)
    outs = pl.pallas_call(
        functools.partial(panel_kernel, s, count),
        grid=(1,),
        out_shape=[jax.ShapeDtypeStruct((n, PW), BF16)] * (2 * count),
        in_specs=[pl.BlockSpec(memory_space=pltpu.SMEM)]
        + [
            pl.BlockSpec((1,) + x.shape[1:], lambda g, i=i: (i, 0, 0), pipeline_mode=pl.Buffered(1)) for x, i in pieces
        ]
        + [full] * len(flat),
        out_specs=[full] * (2 * count),
        scratch_shapes=[pltpu.VMEM((n, PW), F32), pltpu.VMEM((PW, PW), F32)],
        compiler_params=pltpu.CompilerParams(vmem_limit_bytes=VMEM_BYTES),
        cost_estimate=pl.CostEstimate(flops=30 * 10**9 * count, bytes_accessed=10**7, transcendentals=0),
        name="factor_panels",
    )(at, *[x for x, _ in pieces], *flat)
    return [(outs[2 * i], outs[2 * i + 1]) for i in range(count)]


def times_inverse(x, v_refs, store):
    half = PW // 2
    for s in range(len(v_refs) // 2):
        vh, vl = v_refs[2 * s], v_refs[2 * s + 1]
        for h in range(2):
            depth = s * PW + (h + 1) * half
            cols = slice(h * half, (h + 1) * half)
            part = x[:, :depth]
            both = jnp.concatenate([part, part], axis=1)
            v = jnp.concatenate([vh[:depth, cols], vl[:depth, cols]], axis=0)
            store(s * PW + h * half, jnp.dot(both, v, preferred_element_type=F32).astype(BF16))


def v_specs(count):
    specs = []
    for s in range(count):
        spec = pl.BlockSpec(((s + 1) * PW, PW), lambda *_: (0, 0), pipeline_mode=pl.Buffered(1))
        specs += [spec, spec]
    return specs


def solve_kernel(count_ref, order_ref, x0_ref, x1_ref, *refs):
    out_ref = refs[-1]

    @pl.when(2 * pl.program_id(0) < count_ref[0])
    def _():
        def store(at, value):
            out_ref[:, at : at + PW // 2] = value

        times_inverse(jnp.concatenate([x0_ref[0], x1_ref[0]], axis=0), refs[:-1], store)


def solve(x, count, order, panels):
    n = x.shape[2]
    flat = [v for pair in panels for v in pair]
    return pl.pallas_call(
        solve_kernel,
        grid_spec=pltpu.PrefetchScalarGridSpec(
            num_scalar_prefetch=2,
            grid=(4,),
            in_specs=[
                pl.BlockSpec((1, B, n), lambda g, c, o: (o[2 * g], 0, 0)),
                pl.BlockSpec((1, B, n), lambda g, c, o: (o[2 * g + 1], 0, 0)),
            ]
            + v_specs(len(panels)),
            out_specs=pl.BlockSpec((2 * B, n), lambda g, c, o: (g, 0)),
        ),
        out_shape=jax.ShapeDtypeStruct((8 * B, n), BF16),
        compiler_params=pltpu.CompilerParams(vmem_limit_bytes=VMEM_BYTES),
        cost_estimate=pl.CostEstimate(flops=12 * 10**9, bytes_accessed=2 * 10**7, transcendentals=0),
        name="solve",
    )(count, order, x, x, *flat)


def extend_kernel(count_ref, col_ref, row_ref, front_ref, r0_ref, r1_ref, c0_ref, c1_ref, out_ref, prod):
    total = front_ref.shape[0]

    def fill(c, carry):
        rows = pl.ds(pl.multiple_of(c * 1024, 1024), 1024)
        out_ref[rows, :] = front_ref[rows, :].astype(F32)
        return carry

    lax.fori_loop(0, total // 1024, fill, 0)
    for a, (r_ref, c_ref) in enumerate(((r0_ref, c0_ref), (r1_ref, c1_ref))):
        count = count_ref[a]

        def pair(g, carry, a=a, r_ref=r_ref, c_ref=c_ref, count=count):
            right = c_ref[pl.ds(pl.multiple_of(g * 2 * B, 2 * B), 2 * B), :]

            def half(h, inner):
                rows = pl.ds(pl.multiple_of(h * 512, 512), 512)
                prod[rows, :] = dot_t(r_ref[rows, :], right)
                return inner

            lax.fori_loop(0, 2, half, 0)
            for m in range(2):

                @pl.when(2 * g + m < count)
                def _(m=m):
                    slot = col_ref[a, 2 * g + m]
                    for b in range(8):
                        at = pl.ds(row_ref[a, b] * (8 * B) + slot, B, stride=8)
                        out_ref[at, :] = out_ref[at, :] - prod[b * B : (b + 1) * B, m * B : (m + 1) * B]

            return carry

        lax.fori_loop(0, (count + 1) // 2, pair, 0)


def extend(counts, col_slots, row_slots, front, r0, r1, c0, c1):
    smem = pl.BlockSpec(memory_space=pltpu.SMEM)
    vmem = pl.BlockSpec(memory_space=pltpu.VMEM)
    return pl.pallas_call(
        extend_kernel,
        out_shape=jax.ShapeDtypeStruct(front.shape, F32),
        in_specs=[smem] * 3 + [vmem] * 5,
        out_specs=vmem,
        scratch_shapes=[pltpu.VMEM((8 * B, 2 * B), F32)],
        compiler_params=pltpu.CompilerParams(vmem_limit_bytes=VMEM_BYTES),
        name="extend_add",
    )(counts, col_slots, row_slots, front, r0, r1, c0, c1)


def move(x, target):
    def flat(c):
        return int(np.ravel_multi_index(c, SIZES))

    pairs = [(flat(c), flat(target(*c))) for c in np.ndindex(*SIZES)]
    return lax.ppermute(x, AXES, pairs)


def step_z(by):
    return lambda yhi, x, ylo, z, core: (yhi, x, ylo, (z + by) % 4, core)


def step_x(by):
    return lambda yhi, x, ylo, z, core: (yhi, (x + by) % 4, ylo, z, core)


def step_y(by):
    def target(yhi, x, ylo, z, core):
        y = (yhi * 2 + ylo + by) % 4
        return (y // 2, x, y % 2, z, core)

    return target


def step_first(by):
    return lambda *c: (step_x(by) if c[4] == 0 else step_y(by))(*c)


def step_second(by):
    return lambda *c: (step_y(by) if c[4] == 0 else step_x(by))(*c)


def ring(x, step):
    return x, move(x, step(1)), move(x, step(2)), move(x, step(-1))


def after(x, done):
    return lax.optimization_barrier((x, done))


def axis_groups(stage):
    groups = {}
    for c in np.ndindex(*SIZES):
        yhi, x, ylo, z, core = c
        along_x = core == stage
        key = (core, z, yhi, ylo) if along_x else (core, z, x)
        groups.setdefault(key, []).append((x if along_x else yhi * 2 + ylo, int(np.ravel_multi_index(c, SIZES))))
    return [[device for _, device in sorted(group)] for group in groups.values()]


def swap(x):
    return move(x, lambda yhi, x, ylo, z, core: (yhi, x, ylo, z, 1 - core))


def to_col_group(yhi, x, ylo, z, core):
    shift = z if core == 0 else (z + 2) % 4
    y = (yhi * 2 + ylo + shift) % 4
    return (y // 2, x if core == 0 else 3 - x, y % 2, yhi * 2 + x // 2, ylo)


def pick(x, index):
    return lax.dynamic_index_in_dim(x, index, 0, keepdims=False)


def per_device(child_pivot, child_panel, child_map, panel_mask, parent_front):
    yhi, x, ylo, z, core = (lax.axis_index(name) for name in AXES)
    row = yhi * 4 + x
    y = yhi * 2 + ylo
    at = jnp.stack([yhi, x, ylo, z, core]).astype(jnp.int32)
    n = child_pivot.shape[2]
    np_ = n // PW

    other = swap(pick(child_pivot, 1 - core))
    own = pick(child_pivot, core)
    strip = jnp.where(core == 0, jnp.concatenate([own, other]), jnp.concatenate([other, own]))
    strip = strip.reshape(STRIP, np_, PW).transpose(1, 0, 2)

    def plane(part):
        part = jnp.stack(ring(part, step_z), axis=1)
        return jnp.stack(ring(part, step_first), axis=1).reshape(2, 16 * STRIP, PW)

    mask = pick(pick(panel_mask, ylo), row * 8 + z * 2 + core)
    kept = (child_panel.reshape(B, n // B, B) * mask.astype(BF16)[None, :, None]).reshape(B, n)
    first = plane(strip[:2])
    first, kept = after(first, kept)
    for_col = move(kept, to_col_group)
    back, ahead = move(first, step_second(1)), move(first, step_second(-1))
    far = move(back[:1], step_second(1)), move(ahead[1:], step_second(-1))
    rest = plane(after(strip[2:], first)[0])

    maps = child_map.reshape(2, 8, 8)
    maps = jnp.stack([pick(maps, core), pick(maps, 1 - core)])
    slots = maps // 8
    row_slots = lax.dynamic_index_in_dim(slots, row, 1, keepdims=False)
    by_col = lax.dynamic_slice_in_dim(slots, 2 * z, 2, axis=1)
    needed = by_col % 2 == ylo
    place = jnp.cumsum(needed.astype(jnp.int32), axis=2) - 1
    hit = (place[..., None, :] == jnp.arange(8)[:, None]) & needed[..., None, :]
    i = jnp.arange(8)
    from_z, from_core = (i // 2)[None, :], (i % 2)[None, :]
    from_x = 2 * (z % 2) + jnp.arange(2)[:, None]
    x_of = jnp.where(from_core == 0, from_x, 3 - from_x)
    y_of = (2 * (z // 2) + core + from_z + 2 * from_core) % 4 + 0 * x_of
    where = jnp.where(core == 0, y_of * 4 + x_of, x_of * 4 + y_of)
    order = jnp.sum(jnp.where(hit[0], where[:, None, :], 0), axis=2).astype(jnp.int32)
    col_slots = jnp.sum(jnp.where(hit, (by_col // 2)[..., None, :], 0), axis=3).astype(jnp.int32)
    counts = jnp.sum(needed, axis=2).astype(jnp.int32)

    mine_cols = lax.dynamic_index_in_dim(col_slots, core, 1, keepdims=False)
    mine_counts = lax.dynamic_index_in_dim(counts, core, 1, keepdims=False)
    ask_near = (pick(counts[0], 1 - core)[None], pick(order, 1 - core))
    ask_own = (pick(counts[0], core)[None], pick(order, core))
    small = (mine_cols, mine_counts, row_slots, ask_near, ask_own)

    (small, rest, for_col), arrived = after((small, rest, for_col), (back, ahead) + far)
    mine_cols, mine_counts, row_slots, ask_near, ask_own = small
    back, ahead, *far = arrived
    near_rest = move(rest, step_second(1)), move(rest, step_second(-1))
    for_col = lax.all_gather(for_col, AXES, axis=0, axis_index_groups=axis_groups(0))

    panels = factor_panels(0, n, at, [(first, 0), (back, 0), (far[0], 0), (ahead, 0)], [])
    (near_rest, for_col), panels[0] = after((near_rest, for_col), panels[0])
    back2, ahead2 = near_rest
    far2 = move(back2[:1], step_second(1)), move(ahead2[1:], step_second(-1))
    for_col = lax.all_gather(for_col, AXES, axis=0, axis_index_groups=axis_groups(1))
    panels += factor_panels(1, n, at, [(first, 1), (back, 1), (far[1], 0), (ahead, 1)], panels)
    (far2, kept), panels[1] = after((far2, kept), panels[1])
    row_panel = lax.all_gather(kept, ("ylo", "z", "core"), axis=0)
    pieces = [p for i in range(np_ - 2) for p in [(rest, i), (back2, i), (far2[i], 0), (ahead2, i)]]
    panels += factor_panels(2, n, at, pieces, panels)
    col_panel = for_col.reshape(16, B, n)

    col_other = swap(solve(col_panel, *ask_near, panels))
    row_order = core * 8 + jnp.arange(8, dtype=jnp.int32)
    row_side = solve(row_panel, jnp.full((1,), 8, jnp.int32), row_order, panels)
    row_other = swap(row_side)
    row_side, col_panel = after(row_side, col_panel)
    col_own = solve(col_panel, *ask_own, panels)

    front = parent_front.reshape(-1, B)
    out = extend(mine_counts, mine_cols, row_slots, front, row_side, row_other, col_own, col_other)
    return out.reshape(parent_front.shape)


def solution(mesh):
    rows, cols = AXES[:2], AXES[2:]
    split_mesh = Mesh(mesh.devices.reshape(SIZES), AXES)
    front = P(None, rows, None, None, cols, None)
    return jax.shard_map(
        per_device,
        mesh=split_mesh,
        in_specs=(P(None, AXES, None), P(rows, cols, None, None), P(), P(), front),
        out_specs=front,
        check_vma=False,
    )
```

```python
import functools

import jax
import jax.numpy as jnp
import numpy as np
from jax import lax
from jax.experimental import pallas as pl
from jax.experimental.pallas import tpu as pltpu
from jax.sharding import Mesh, PartitionSpec as P

F32 = jnp.float32
BF16 = jnp.bfloat16
B = 128
PW = 512
VMEM_BYTES = 56 << 20
STRIP = 32
AXES = ("yhi", "x", "ylo", "z", "core")
SIZES = (2, 4, 2, 4, 2)


def split(x):
    hi = x.astype(BF16)
    return hi, (x - hi.astype(F32)).astype(BF16)


def dot_t(x, y):
    return lax.dot_general(x, y, (((1,), (1,)), ((), ())), preferred_element_type=F32)


def dot3_t(xh, xl, yh, yl):
    return dot_t(jnp.concatenate([xh, xh, xl], axis=1), jnp.concatenate([yh, yl, yh], axis=1))


def leaf_inverse(block):
    lane = lax.broadcasted_iota(jnp.int32, (8, B), 1)
    sub = lax.broadcasted_iota(jnp.int32, (8, B), 0)
    groups = B // 8
    rows = [block[8 * i : 8 * i + 8, :] for i in range(groups)]

    def row_of(x, j):
        return jnp.broadcast_to(x[j : j + 1, :], (8, B))

    def col_of(x, j):
        return jnp.broadcast_to(x[:, j : j + 1], (8, B))

    def total(p):
        return ((p[0] + p[1]) + (p[2] + p[3])) + ((p[4] + p[5]) + (p[6] + p[7]))

    done = []
    cols = [col_of(rows[0], j) for j in range(8)]
    for t in range(groups):
        lo = 8 * t
        rel = lane - lo
        inside = (rel >= 0) & (rel < 8)
        last = t == groups - 1
        if not last:
            ahead = [col_of(rows[t], lo + 8 + j) for j in range(8)]
            below = [col_of(rows[t + 1], lo + 8 + j) for j in range(8)]
            left = [col_of(rows[t + 1], lo + j) for j in range(8)]
        half = jnp.where(inside, jnp.where(rel == sub, 1.0, 0.0), rows[t])
        full = half
        pivots = jnp.ones((8, B), F32)
        recips = jnp.ones((8, B), F32)
        for j in range(8):
            pivot = row_of(cols[j], j)
            recip = pltpu.reciprocal(pivot, approx=True)
            pivots = jnp.where(sub == j, pivot, pivots)
            recips = jnp.where(sub == j, recip, recips)
            mult = jnp.where(sub != j, cols[j], 0.0) * recip
            for jj in range(j + 1, 8):
                cols[jj] = cols[jj] - mult * row_of(cols[jj], j)
            row = row_of(half, j)
            half = half - jnp.where(sub > j, mult, 0.0) * row
            full = full - mult * row
            if not last:
                ahead = [c - mult * row_of(c, j) for c in ahead]
        full = full * recips
        done.append(jnp.where(lane <= sub + lo, half * lax.rsqrt(pivots), 0.0))
        if last:
            break
        ahead = [c * recips for c in ahead]
        cols = [b - total([left[j] * row_of(c, j) for j in range(8)]) for b, c in zip(below, ahead)]
        rows[t + 1] = jnp.where(inside, 0.0, rows[t + 1]) - total([left[j] * row_of(full, j) for j in range(8)])
        if t + 2 < groups:
            lh, ll = split(jnp.concatenate([jnp.where(inside, r, 0.0) for r in rows[t + 2 :]], axis=0))
            zero = jnp.zeros((8, B), F32)
            fh, fl = split(jnp.concatenate([full if i == t else zero for i in range(groups)], axis=0))
            less = jnp.dot(
                jnp.concatenate([lh, lh, ll], axis=1),
                jnp.concatenate([fh, fl, fh], axis=0),
                preferred_element_type=F32,
            )
            for i in range(t + 2, groups):
                rows[i] = jnp.where(inside, 0.0, rows[i]) - less[8 * (i - t - 2) : 8 * (i - t - 1)]
    return jnp.concatenate(done, axis=0)


def place_strips(s, at_ref, pieces, work):
    yhi, x, ylo, z, core = (at_ref[i] for i in range(5))
    y = yhi * 2 + ylo
    for far, ref in enumerate(pieces):

        def strip(g, carry, ref=ref, far=far):
            mid, near = g // 4, g % 4
            xx = (x - jnp.where(core == 0, mid, far)) & 3
            yy = (y - jnp.where(core == 0, far, mid)) & 3
            zz = (z - near) & 3
            row = ((yy // 2) * 4 + xx) * 8 + (yy % 2) * 4 + zz
            rows = pl.ds(pl.multiple_of(g * STRIP, STRIP), STRIP)
            to = pl.ds(pl.multiple_of(row * STRIP, STRIP), STRIP)

            @pl.when(row >= s * PW // STRIP)
            def _():
                work[to, :] = ref[0, rows, :].astype(F32)

            return carry

        lax.fori_loop(0, ref.shape[1] // STRIP, strip, 0)


def panel_kernel(s, count, at_ref, *refs):
    pieces, refs = refs[: 4 * count], refs[4 * count :]
    prev = [(refs[2 * p], refs[2 * p + 1]) for p in range(s + count)]
    work, square = refs[2 * (s + count) :]
    for i in range(count):
        one_panel(s + i, at_ref, pieces[4 * i : 4 * i + 4], prev[: s + i], *prev[s + i], work, square)


def one_panel(s, at_ref, pieces, prev, hi_ref, lo_ref, work, square):
    n = work.shape[0]
    base = s * PW
    place_strips(s, at_ref, pieces, work)

    def load(pair, rows):
        return pair[0][rows, :], pair[1][rows, :]

    right = [load(pair, pl.ds(base, PW)) for pair in prev]

    def left(rows, p):
        return dot3_t(*load(prev[p], rows), *right[p])

    def own_rows(c, carry):
        rows = pl.ds(pl.multiple_of(base + c * 256, 256), 256)
        total = work[rows, :]
        for p in range(s):
            total = total - left(rows, p)
        square[pl.ds(pl.multiple_of(c * 256, 256), 256), :] = total
        return carry

    lax.fori_loop(0, PW // 256, own_rows, 0)

    def other_rows(k):
        if s == 0:
            return
        count = (n - PW) // (4 * B)
        at = [k * ((n - PW) // 4) + i * B for i in range(count)]
        at = [jnp.where(row < base, row, row + PW) for row in at]
        rows = [pl.ds(pl.multiple_of(row, B), B) for row in at]
        total = jnp.concatenate([jnp.where(row > base, work[r, :], 0.0) for row, r in zip(at, rows)], axis=0)
        for p in range(s):
            part = [load(prev[p], r) for r in rows]
            product = dot3_t(*[jnp.concatenate(half, axis=0) for half in zip(*part)], *right[p])
            use = [(row > base) | (row < (p + 1) * PW) for row in at]
            use = [jnp.broadcast_to(u.astype(F32), (B, PW)) for u in use]
            total = total - product * jnp.concatenate(use, axis=0)
        for i, r in enumerate(rows):
            work[r, :] = total[i * B : (i + 1) * B]

    eye = (lax.broadcasted_iota(jnp.int32, (B, B), 0) == lax.broadcasted_iota(jnp.int32, (B, B), 1)).astype(F32)

    def step(k, carry):
        cols = pl.ds(pl.multiple_of(k * B, B), B)
        block = square[cols, cols]
        other_rows(k)
        inv = leaf_inverse(block)
        square[cols, cols] = eye
        qh, ql = split(dot3_t(*split(square[:, cols]), *split(inv)))
        hi_ref[pl.ds(base, PW), cols] = qh
        lo_ref[pl.ds(base, PW), cols] = ql
        for kk in range(PW // B - 1):

            @pl.when(k == kk)
            def _(kk=kk):
                width = PW - (kk + 1) * B
                at = pl.ds(kk * B, B)
                later = pl.ds((kk + 1) * B, width)
                below = pl.ds(base + (kk + 1) * B, width)
                square[at, later] = jnp.zeros((B, width), F32)
                yh, yl = hi_ref[below, at], lo_ref[below, at]
                qh, ql = hi_ref[pl.ds(base, PW), at], lo_ref[pl.ds(base, PW), at]
                square[:, later] = square[:, later] - dot3_t(qh, ql, yh, yl)
                hi_ref[below, at] = jnp.zeros((width, B), BF16)
                lo_ref[below, at] = jnp.zeros((width, B), BF16)

        return carry

    lax.fori_loop(0, PW // B, step, 0)
    half = PW // 2
    parts = []
    for h in range(2):
        at = pl.ds(base, (h + 1) * half), pl.ds(h * half, half)
        vh, vl = hi_ref[at], lo_ref[at]
        parts.append(jnp.concatenate([vh, vl, vh], axis=0))
    for rb in range(n // PW):
        if rb != s:

            def rest(c, carry, rb=rb):
                rows = pl.ds(pl.multiple_of(rb * PW + c * 256, 256), 256)
                xh, xl = split(work[rows, :])
                for h in range(2):
                    ah, al = xh[:, : (h + 1) * half], xl[:, : (h + 1) * half]
                    q = jnp.dot(jnp.concatenate([ah, ah, al], axis=1), parts[h], preferred_element_type=F32)
                    cols = pl.ds(h * half, half)
                    hi_ref[rows, cols], lo_ref[rows, cols] = split(q)
                return carry

            lax.fori_loop(0, PW // 256, rest, 0)


def factor_panels(s, n, at, pieces, prev):
    count = len(pieces) // 4
    flat = [x for pair in prev for x in pair]
    full = pl.BlockSpec(memory_space=pltpu.VMEM)
    outs = pl.pallas_call(
        functools.partial(panel_kernel, s, count),
        grid=(1,),
        out_shape=[jax.ShapeDtypeStruct((n, PW), BF16)] * (2 * count),
        in_specs=[pl.BlockSpec(memory_space=pltpu.SMEM)]
        + [
            pl.BlockSpec((1,) + x.shape[1:], lambda g, i=i: (i, 0, 0), pipeline_mode=pl.Buffered(1)) for x, i in pieces
        ]
        + [full] * len(flat),
        out_specs=[full] * (2 * count),
        scratch_shapes=[pltpu.VMEM((n, PW), F32), pltpu.VMEM((PW, PW), F32)],
        compiler_params=pltpu.CompilerParams(vmem_limit_bytes=VMEM_BYTES),
        cost_estimate=pl.CostEstimate(flops=30 * 10**9 * count, bytes_accessed=10**7, transcendentals=0),
        name="factor_panels",
    )(at, *[x for x, _ in pieces], *flat)
    return [(outs[2 * i], outs[2 * i + 1]) for i in range(count)]


def times_inverse(x, v_refs, store):
    half = PW // 2
    for s in range(len(v_refs) // 2):
        vh, vl = v_refs[2 * s], v_refs[2 * s + 1]
        for h in range(2):
            depth = s * PW + (h + 1) * half
            cols = slice(h * half, (h + 1) * half)
            part = x[:, :depth]
            both = jnp.concatenate([part, part], axis=1)
            v = jnp.concatenate([vh[:depth, cols], vl[:depth, cols]], axis=0)
            store(s * PW + h * half, jnp.dot(both, v, preferred_element_type=F32).astype(BF16))


def v_specs(count):
    specs = []
    for s in range(count):
        spec = pl.BlockSpec(((s + 1) * PW, PW), lambda *_: (0, 0), pipeline_mode=pl.Buffered(1))
        specs += [spec, spec]
    return specs


def solve_kernel(count_ref, order_ref, x0_ref, x1_ref, *refs):
    out_ref = refs[-1]

    @pl.when(2 * pl.program_id(0) < count_ref[0])
    def _():
        def store(at, value):
            out_ref[:, at : at + PW // 2] = value

        times_inverse(jnp.concatenate([x0_ref[0], x1_ref[0]], axis=0), refs[:-1], store)


def solve(x, count, order, panels):
    n = x.shape[2]
    flat = [v for pair in panels for v in pair]
    return pl.pallas_call(
        solve_kernel,
        grid_spec=pltpu.PrefetchScalarGridSpec(
            num_scalar_prefetch=2,
            grid=(4,),
            in_specs=[
                pl.BlockSpec((1, B, n), lambda g, c, o: (o[2 * g], 0, 0)),
                pl.BlockSpec((1, B, n), lambda g, c, o: (o[2 * g + 1], 0, 0)),
            ]
            + v_specs(len(panels)),
            out_specs=pl.BlockSpec((2 * B, n), lambda g, c, o: (g, 0)),
        ),
        out_shape=jax.ShapeDtypeStruct((8 * B, n), BF16),
        compiler_params=pltpu.CompilerParams(vmem_limit_bytes=VMEM_BYTES),
        cost_estimate=pl.CostEstimate(flops=12 * 10**9, bytes_accessed=2 * 10**7, transcendentals=0),
        name="solve",
    )(count, order, x, x, *flat)


def extend_kernel(count_ref, col_ref, row_ref, front_ref, r0_ref, r1_ref, c0_ref, c1_ref, out_ref, prod):
    total = front_ref.shape[0]

    def fill(c, carry):
        rows = pl.ds(pl.multiple_of(c * 1024, 1024), 1024)
        out_ref[rows, :] = front_ref[rows, :].astype(F32)
        return carry

    lax.fori_loop(0, total // 1024, fill, 0)
    for a, (r_ref, c_ref) in enumerate(((r0_ref, c0_ref), (r1_ref, c1_ref))):
        count = count_ref[a]

        def pair(g, carry, a=a, r_ref=r_ref, c_ref=c_ref, count=count):
            right = c_ref[pl.ds(pl.multiple_of(g * 2 * B, 2 * B), 2 * B), :]

            def half(h, inner):
                rows = pl.ds(pl.multiple_of(h * 512, 512), 512)
                prod[rows, :] = dot_t(r_ref[rows, :], right)
                return inner

            lax.fori_loop(0, 2, half, 0)
            for m in range(2):

                @pl.when(2 * g + m < count)
                def _(m=m):
                    slot = col_ref[a, 2 * g + m]
                    for b in range(8):
                        at = pl.ds(row_ref[a, b] * (8 * B) + slot, B, stride=8)
                        out_ref[at, :] = out_ref[at, :] - prod[b * B : (b + 1) * B, m * B : (m + 1) * B]

            return carry

        lax.fori_loop(0, (count + 1) // 2, pair, 0)


def extend(counts, col_slots, row_slots, front, r0, r1, c0, c1):
    smem = pl.BlockSpec(memory_space=pltpu.SMEM)
    vmem = pl.BlockSpec(memory_space=pltpu.VMEM)
    return pl.pallas_call(
        extend_kernel,
        out_shape=jax.ShapeDtypeStruct(front.shape, F32),
        in_specs=[smem] * 3 + [vmem] * 5,
        out_specs=vmem,
        scratch_shapes=[pltpu.VMEM((8 * B, 2 * B), F32)],
        compiler_params=pltpu.CompilerParams(vmem_limit_bytes=VMEM_BYTES),
        name="extend_add",
    )(counts, col_slots, row_slots, front, r0, r1, c0, c1)


def move(x, target):
    def flat(c):
        return int(np.ravel_multi_index(c, SIZES))

    pairs = [(flat(c), flat(target(*c))) for c in np.ndindex(*SIZES)]
    return lax.ppermute(x, AXES, pairs)


def step_z(by):
    return lambda yhi, x, ylo, z, core: (yhi, x, ylo, (z + by) % 4, core)


def step_x(by):
    return lambda yhi, x, ylo, z, core: (yhi, (x + by) % 4, ylo, z, core)


def step_y(by):
    def target(yhi, x, ylo, z, core):
        y = (yhi * 2 + ylo + by) % 4
        return (y // 2, x, y % 2, z, core)

    return target


def step_first(by):
    return lambda *c: (step_x(by) if c[4] == 0 else step_y(by))(*c)


def step_second(by):
    return lambda *c: (step_y(by) if c[4] == 0 else step_x(by))(*c)


def ring(x, step):
    return x, move(x, step(1)), move(x, step(2)), move(x, step(-1))


def after(x, done):
    return lax.optimization_barrier((x, done))


def axis_groups(stage):
    groups = {}
    for c in np.ndindex(*SIZES):
        yhi, x, ylo, z, core = c
        along_x = core == stage
        key = (core, z, yhi, ylo) if along_x else (core, z, x)
        groups.setdefault(key, []).append((x if along_x else yhi * 2 + ylo, int(np.ravel_multi_index(c, SIZES))))
    return [[device for _, device in sorted(group)] for group in groups.values()]


def swap(x):
    return move(x, lambda yhi, x, ylo, z, core: (yhi, x, ylo, z, 1 - core))


def to_col_group(yhi, x, ylo, z, core):
    shift = z if core == 0 else (z + 2) % 4
    y = (yhi * 2 + ylo + shift) % 4
    return (y // 2, x if core == 0 else 3 - x, y % 2, yhi * 2 + x // 2, ylo)


def pick(x, index):
    return lax.dynamic_index_in_dim(x, index, 0, keepdims=False)


def per_device(child_pivot, child_panel, child_map, panel_mask, parent_front):
    yhi, x, ylo, z, core = (lax.axis_index(name) for name in AXES)
    row = yhi * 4 + x
    y = yhi * 2 + ylo
    at = jnp.stack([yhi, x, ylo, z, core]).astype(jnp.int32)
    n = child_pivot.shape[2]
    np_ = n // PW

    other = swap(pick(child_pivot, 1 - core))
    own = pick(child_pivot, core)
    strip = jnp.where(core == 0, jnp.concatenate([own, other]), jnp.concatenate([other, own]))
    strip = strip.reshape(STRIP, np_, PW).transpose(1, 0, 2)

    parts = ring(strip, step_z)

    def plane(near):
        return jnp.stack(ring(near, step_first), axis=1).reshape(2, 16 * STRIP, PW)

    mask = pick(pick(panel_mask, ylo), row * 8 + z * 2 + core)
    kept = (child_panel.reshape(B, n // B, B) * mask.astype(BF16)[None, :, None]).reshape(B, n)
    first = plane(jnp.stack([part[:2] for part in parts], axis=1))
    first, kept = after(first, kept)
    for_col = move(kept, to_col_group)
    back, ahead = move(first, step_second(1)), move(first, step_second(-1))
    far = move(back[:1], step_second(1)), move(ahead[1:], step_second(-1))
    rest = plane(after(jnp.stack([part[2:] for part in parts], axis=1), first)[0])

    maps = child_map.reshape(2, 8, 8)
    maps = jnp.stack([pick(maps, core), pick(maps, 1 - core)])
    slots = maps // 8
    row_slots = lax.dynamic_index_in_dim(slots, row, 1, keepdims=False)
    by_col = lax.dynamic_slice_in_dim(slots, 2 * z, 2, axis=1)
    needed = by_col % 2 == ylo
    place = jnp.cumsum(needed.astype(jnp.int32), axis=2) - 1
    hit = (place[..., None, :] == jnp.arange(8)[:, None]) & needed[..., None, :]
    i = jnp.arange(8)
    from_z, from_core = (i // 2)[None, :], (i % 2)[None, :]
    from_x = 2 * (z % 2) + jnp.arange(2)[:, None]
    x_of = jnp.where(from_core == 0, from_x, 3 - from_x)
    y_of = (2 * (z // 2) + core + from_z + 2 * from_core) % 4 + 0 * x_of
    where = jnp.where(core == 0, y_of * 4 + x_of, x_of * 4 + y_of)
    order = jnp.sum(jnp.where(hit[0], where[:, None, :], 0), axis=2).astype(jnp.int32)
    col_slots = jnp.sum(jnp.where(hit, (by_col // 2)[..., None, :], 0), axis=3).astype(jnp.int32)
    counts = jnp.sum(needed, axis=2).astype(jnp.int32)

    mine_cols = lax.dynamic_index_in_dim(col_slots, core, 1, keepdims=False)
    mine_counts = lax.dynamic_index_in_dim(counts, core, 1, keepdims=False)
    ask_near = (pick(counts[0], 1 - core)[None], pick(order, 1 - core))
    ask_own = (pick(counts[0], core)[None], pick(order, core))
    small = (mine_cols, mine_counts, row_slots, ask_near, ask_own)

    (small, rest, for_col), arrived = after((small, rest, for_col), (back, ahead) + far)
    mine_cols, mine_counts, row_slots, ask_near, ask_own = small
    back, ahead, *far = arrived
    near_rest = move(rest, step_second(1)), move(rest, step_second(-1))
    for_col = lax.all_gather(for_col, AXES, axis=0, axis_index_groups=axis_groups(0))

    panels = factor_panels(0, n, at, [(first, 0), (back, 0), (far[0], 0), (ahead, 0)], [])
    (near_rest, for_col), panels[0] = after((near_rest, for_col), panels[0])
    back2, ahead2 = near_rest
    far2 = move(back2[:1], step_second(1)), move(ahead2[1:], step_second(-1))
    for_col = lax.all_gather(for_col, AXES, axis=0, axis_index_groups=axis_groups(1))
    panels += factor_panels(1, n, at, [(first, 1), (back, 1), (far[1], 0), (ahead, 1)], panels)
    (far2, kept), panels[1] = after((far2, kept), panels[1])
    row_panel = lax.all_gather(kept, ("ylo", "z", "core"), axis=0)
    pieces = [p for i in range(np_ - 2) for p in [(rest, i), (back2, i), (far2[i], 0), (ahead2, i)]]
    panels += factor_panels(2, n, at, pieces, panels)
    col_panel = for_col.reshape(16, B, n)

    col_other = swap(solve(col_panel, *ask_near, panels))
    row_order = core * 8 + jnp.arange(8, dtype=jnp.int32)
    row_side = solve(row_panel, jnp.full((1,), 8, jnp.int32), row_order, panels)
    row_other = swap(row_side)
    row_side, col_panel = after(row_side, col_panel)
    col_own = solve(col_panel, *ask_own, panels)

    front = parent_front.reshape(-1, B)
    out = extend(mine_counts, mine_cols, row_slots, front, row_side, row_other, col_own, col_other)
    return out.reshape(parent_front.shape)


def solution(mesh):
    rows, cols = AXES[:2], AXES[2:]
    split_mesh = Mesh(mesh.devices.reshape(SIZES), AXES)
    front = P(None, rows, None, None, cols, None)
    return jax.shard_map(
        per_device,
        mesh=split_mesh,
        in_specs=(P(None, AXES, None), P(rows, cols, None, None), P(), P(), front),
        out_specs=front,
        check_vma=False,
    )
```

```python
import functools

import jax
import jax.numpy as jnp
import numpy as np
from jax import lax
from jax.experimental import pallas as pl
from jax.experimental.pallas import tpu as pltpu
from jax.sharding import Mesh, PartitionSpec as P

F32 = jnp.float32
BF16 = jnp.bfloat16
B = 128
PW = 512
VMEM_BYTES = 56 << 20
STRIP = 32
AXES = ("yhi", "x", "ylo", "z", "core")
SIZES = (2, 4, 2, 4, 2)


def split(x):
    hi = x.astype(BF16)
    return hi, (x - hi.astype(F32)).astype(BF16)


def dot_t(x, y):
    return lax.dot_general(x, y, (((1,), (1,)), ((), ())), preferred_element_type=F32)


def dot3_t(xh, xl, yh, yl):
    return dot_t(jnp.concatenate([xh, xh, xl], axis=1), jnp.concatenate([yh, yl, yh], axis=1))


def leaf_inverse(block):
    lane = lax.broadcasted_iota(jnp.int32, (8, B), 1)
    sub = lax.broadcasted_iota(jnp.int32, (8, B), 0)
    groups = B // 8
    rows = [block[8 * i : 8 * i + 8, :] for i in range(groups)]

    def row_of(x, j):
        return jnp.broadcast_to(x[j : j + 1, :], (8, B))

    def col_of(x, j):
        return jnp.broadcast_to(x[:, j : j + 1], (8, B))

    def total(p):
        return ((p[0] + p[1]) + (p[2] + p[3])) + ((p[4] + p[5]) + (p[6] + p[7]))

    done = []
    cols = [col_of(rows[0], j) for j in range(8)]
    for t in range(groups):
        lo = 8 * t
        rel = lane - lo
        inside = (rel >= 0) & (rel < 8)
        last = t == groups - 1
        if not last:
            ahead = [col_of(rows[t], lo + 8 + j) for j in range(8)]
            below = [col_of(rows[t + 1], lo + 8 + j) for j in range(8)]
            left = [col_of(rows[t + 1], lo + j) for j in range(8)]
        half = jnp.where(inside, jnp.where(rel == sub, 1.0, 0.0), rows[t])
        full = half
        pivots = jnp.ones((8, B), F32)
        recips = jnp.ones((8, B), F32)
        for j in range(8):
            pivot = row_of(cols[j], j)
            recip = pltpu.reciprocal(pivot, approx=True)
            pivots = jnp.where(sub == j, pivot, pivots)
            recips = jnp.where(sub == j, recip, recips)
            mult = jnp.where(sub != j, cols[j], 0.0) * recip
            for jj in range(j + 1, 8):
                cols[jj] = cols[jj] - mult * row_of(cols[jj], j)
            row = row_of(half, j)
            half = half - jnp.where(sub > j, mult, 0.0) * row
            full = full - mult * row
            if not last:
                ahead = [c - mult * row_of(c, j) for c in ahead]
        full = full * recips
        done.append(jnp.where(lane <= sub + lo, half * lax.rsqrt(pivots), 0.0))
        if last:
            break
        ahead = [c * recips for c in ahead]
        cols = [b - total([left[j] * row_of(c, j) for j in range(8)]) for b, c in zip(below, ahead)]
        rows[t + 1] = jnp.where(inside, 0.0, rows[t + 1]) - total([left[j] * row_of(full, j) for j in range(8)])
        if t + 2 < groups:
            lh, ll = split(jnp.concatenate([jnp.where(inside, r, 0.0) for r in rows[t + 2 :]], axis=0))
            zero = jnp.zeros((8, B), F32)
            fh, fl = split(jnp.concatenate([full if i == t else zero for i in range(groups)], axis=0))
            less = jnp.dot(
                jnp.concatenate([lh, lh, ll], axis=1),
                jnp.concatenate([fh, fl, fh], axis=0),
                preferred_element_type=F32,
            )
            for i in range(t + 2, groups):
                rows[i] = jnp.where(inside, 0.0, rows[i]) - less[8 * (i - t - 2) : 8 * (i - t - 1)]
    return jnp.concatenate(done, axis=0)


def place_strips(s, at_ref, pieces, work):
    yhi, x, ylo, z, core = (at_ref[i] for i in range(5))
    y = yhi * 2 + ylo
    for far, ref in enumerate(pieces):

        def strip(g, carry, ref=ref, far=far):
            mid, near = g // 4, g % 4
            xx = (x - jnp.where(core == 0, mid, far)) & 3
            yy = (y - jnp.where(core == 0, far, mid)) & 3
            zz = (z - near) & 3
            row = ((yy // 2) * 4 + xx) * 8 + (yy % 2) * 4 + zz
            rows = pl.ds(pl.multiple_of(g * STRIP, STRIP), STRIP)
            to = pl.ds(pl.multiple_of(row * STRIP, STRIP), STRIP)

            @pl.when(row >= s * PW // STRIP)
            def _():
                work[to, :] = ref[0, rows, :].astype(F32)

            return carry

        lax.fori_loop(0, ref.shape[1] // STRIP, strip, 0)


def panel_kernel(s, count, at_ref, *refs):
    pieces, refs = refs[: 4 * count], refs[4 * count :]
    prev = [(refs[2 * p], refs[2 * p + 1]) for p in range(s + count)]
    work, square = refs[2 * (s + count) :]
    for i in range(count):
        one_panel(s + i, at_ref, pieces[4 * i : 4 * i + 4], prev[: s + i], *prev[s + i], work, square)


def one_panel(s, at_ref, pieces, prev, hi_ref, lo_ref, work, square):
    n = work.shape[0]
    base = s * PW
    place_strips(s, at_ref, pieces, work)

    def load(pair, rows):
        return pair[0][rows, :], pair[1][rows, :]

    right = [load(pair, pl.ds(base, PW)) for pair in prev]

    def left(rows, p):
        return dot3_t(*load(prev[p], rows), *right[p])

    def own_rows(c, carry):
        rows = pl.ds(pl.multiple_of(base + c * 256, 256), 256)
        total = work[rows, :]
        for p in range(s):
            total = total - left(rows, p)
        square[pl.ds(pl.multiple_of(c * 256, 256), 256), :] = total
        return carry

    lax.fori_loop(0, PW // 256, own_rows, 0)

    def other_rows(k):
        if s == 0:
            return
        count = (n - PW) // (4 * B)
        at = [k * ((n - PW) // 4) + i * B for i in range(count)]
        at = [jnp.where(row < base, row, row + PW) for row in at]
        rows = [pl.ds(pl.multiple_of(row, B), B) for row in at]
        total = jnp.concatenate([jnp.where(row > base, work[r, :], 0.0) for row, r in zip(at, rows)], axis=0)
        for p in range(s):
            part = [load(prev[p], r) for r in rows]
            product = dot3_t(*[jnp.concatenate(half, axis=0) for half in zip(*part)], *right[p])
            use = [(row > base) | (row < (p + 1) * PW) for row in at]
            use = [jnp.broadcast_to(u.astype(F32), (B, PW)) for u in use]
            total = total - product * jnp.concatenate(use, axis=0)
        for i, r in enumerate(rows):
            work[r, :] = total[i * B : (i + 1) * B]

    eye = (lax.broadcasted_iota(jnp.int32, (B, B), 0) == lax.broadcasted_iota(jnp.int32, (B, B), 1)).astype(F32)

    def step(k, carry):
        cols = pl.ds(pl.multiple_of(k * B, B), B)
        block = square[cols, cols]
        other_rows(k)
        inv = leaf_inverse(block)
        square[cols, cols] = eye
        qh, ql = split(dot3_t(*split(square[:, cols]), *split(inv)))
        hi_ref[pl.ds(base, PW), cols] = qh
        lo_ref[pl.ds(base, PW), cols] = ql
        for kk in range(PW // B - 1):

            @pl.when(k == kk)
            def _(kk=kk):
                width = PW - (kk + 1) * B
                at = pl.ds(kk * B, B)
                later = pl.ds((kk + 1) * B, width)
                below = pl.ds(base + (kk + 1) * B, width)
                square[at, later] = jnp.zeros((B, width), F32)
                yh, yl = hi_ref[below, at], lo_ref[below, at]
                qh, ql = hi_ref[pl.ds(base, PW), at], lo_ref[pl.ds(base, PW), at]
                square[:, later] = square[:, later] - dot3_t(qh, ql, yh, yl)
                hi_ref[below, at] = jnp.zeros((width, B), BF16)
                lo_ref[below, at] = jnp.zeros((width, B), BF16)

        return carry

    lax.fori_loop(0, PW // B, step, 0)
    half = PW // 2
    parts = []
    for h in range(2):
        at = pl.ds(base, (h + 1) * half), pl.ds(h * half, half)
        vh, vl = hi_ref[at], lo_ref[at]
        parts.append(jnp.concatenate([vh, vl, vh], axis=0))
    for rb in range(n // PW):
        if rb != s:

            def rest(c, carry, rb=rb):
                rows = pl.ds(pl.multiple_of(rb * PW + c * 256, 256), 256)
                xh, xl = split(work[rows, :])
                for h in range(2):
                    ah, al = xh[:, : (h + 1) * half], xl[:, : (h + 1) * half]
                    q = jnp.dot(jnp.concatenate([ah, ah, al], axis=1), parts[h], preferred_element_type=F32)
                    cols = pl.ds(h * half, half)
                    hi_ref[rows, cols], lo_ref[rows, cols] = split(q)
                return carry

            lax.fori_loop(0, PW // 256, rest, 0)


def factor_panels(s, n, at, pieces, prev):
    count = len(pieces) // 4
    flat = [x for pair in prev for x in pair]
    full = pl.BlockSpec(memory_space=pltpu.VMEM)
    outs = pl.pallas_call(
        functools.partial(panel_kernel, s, count),
        grid=(1,),
        out_shape=[jax.ShapeDtypeStruct((n, PW), BF16)] * (2 * count),
        in_specs=[pl.BlockSpec(memory_space=pltpu.SMEM)]
        + [
            pl.BlockSpec((1,) + x.shape[1:], lambda g, i=i: (i, 0, 0), pipeline_mode=pl.Buffered(1)) for x, i in pieces
        ]
        + [full] * len(flat),
        out_specs=[full] * (2 * count),
        scratch_shapes=[pltpu.VMEM((n, PW), F32), pltpu.VMEM((PW, PW), F32)],
        compiler_params=pltpu.CompilerParams(vmem_limit_bytes=VMEM_BYTES),
        cost_estimate=pl.CostEstimate(flops=30 * 10**9 * count, bytes_accessed=10**7, transcendentals=0),
        name="factor_panels",
    )(at, *[x for x, _ in pieces], *flat)
    return [(outs[2 * i], outs[2 * i + 1]) for i in range(count)]


def times_inverse(x, v_refs, store):
    half = PW // 2
    for s in range(len(v_refs) // 2):
        vh, vl = v_refs[2 * s], v_refs[2 * s + 1]
        for h in range(2):
            depth = s * PW + (h + 1) * half
            cols = slice(h * half, (h + 1) * half)
            part = x[:, :depth]
            both = jnp.concatenate([part, part], axis=1)
            v = jnp.concatenate([vh[:depth, cols], vl[:depth, cols]], axis=0)
            store(s * PW + h * half, jnp.dot(both, v, preferred_element_type=F32).astype(BF16))


def v_specs(count):
    specs = []
    for s in range(count):
        spec = pl.BlockSpec(((s + 1) * PW, PW), lambda *_: (0, 0), pipeline_mode=pl.Buffered(1))
        specs += [spec, spec]
    return specs


def solve_kernel(count_ref, order_ref, x0_ref, x1_ref, *refs):
    out_ref = refs[-1]

    @pl.when(2 * pl.program_id(0) < count_ref[0])
    def _():
        def store(at, value):
            out_ref[:, at : at + PW // 2] = value

        times_inverse(jnp.concatenate([x0_ref[0], x1_ref[0]], axis=0), refs[:-1], store)


def solve(x, count, order, panels):
    n = x.shape[2]
    flat = [v for pair in panels for v in pair]
    return pl.pallas_call(
        solve_kernel,
        grid_spec=pltpu.PrefetchScalarGridSpec(
            num_scalar_prefetch=2,
            grid=(4,),
            in_specs=[
                pl.BlockSpec((1, B, n), lambda g, c, o: (o[2 * g], 0, 0)),
                pl.BlockSpec((1, B, n), lambda g, c, o: (o[2 * g + 1], 0, 0)),
            ]
            + v_specs(len(panels)),
            out_specs=pl.BlockSpec((2 * B, n), lambda g, c, o: (g, 0)),
        ),
        out_shape=jax.ShapeDtypeStruct((8 * B, n), BF16),
        compiler_params=pltpu.CompilerParams(vmem_limit_bytes=VMEM_BYTES),
        cost_estimate=pl.CostEstimate(flops=12 * 10**9, bytes_accessed=2 * 10**7, transcendentals=0),
        name="solve",
    )(count, order, x, x, *flat)


def solve_both_kernel(count_ref, order_ref, x0_ref, x1_ref, *refs):
    outs = refs[-2:]
    e, g = pl.program_id(0), pl.program_id(1)
    for which in range(2):

        @pl.when((e == which) & (2 * g < count_ref[which]))
        def _(which=which):
            def store(at, value):
                outs[which][:, at : at + PW // 2] = value

            times_inverse(jnp.concatenate([x0_ref[0], x1_ref[0]], axis=0), refs[:-2], store)


def solve_both(x, counts, orders, panels):
    n = x.shape[2]
    flat = [v for pair in panels for v in pair]
    out = jax.ShapeDtypeStruct((8 * B, n), BF16)
    return pl.pallas_call(
        solve_both_kernel,
        grid_spec=pltpu.PrefetchScalarGridSpec(
            num_scalar_prefetch=2,
            grid=(2, 4),
            in_specs=[
                pl.BlockSpec((1, B, n), lambda e, g, c, o: (o[e, 2 * g], 0, 0)),
                pl.BlockSpec((1, B, n), lambda e, g, c, o: (o[e, 2 * g + 1], 0, 0)),
            ]
            + v_specs(len(panels)),
            out_specs=[
                pl.BlockSpec((2 * B, n), lambda e, g, c, o: (g + e * (3 - g), 0)),
                pl.BlockSpec((2 * B, n), lambda e, g, c, o: (e * g, 0)),
            ],
        ),
        out_shape=[out, out],
        compiler_params=pltpu.CompilerParams(vmem_limit_bytes=VMEM_BYTES),
        cost_estimate=pl.CostEstimate(flops=24 * 10**9, bytes_accessed=3 * 10**7, transcendentals=0),
        name="solve_both",
    )(counts, orders, x, x, *flat)


def extend_kernel(count_ref, col_ref, row_ref, front_ref, r0_ref, r1_ref, c0_ref, c1_ref, out_ref, prod):
    total = front_ref.shape[0]

    def fill(c, carry):
        rows = pl.ds(pl.multiple_of(c * 1024, 1024), 1024)
        out_ref[rows, :] = front_ref[rows, :].astype(F32)
        return carry

    lax.fori_loop(0, total // 1024, fill, 0)
    for a, (r_ref, c_ref) in enumerate(((r0_ref, c0_ref), (r1_ref, c1_ref))):
        count = count_ref[a]

        def pair(g, carry, a=a, r_ref=r_ref, c_ref=c_ref, count=count):
            right = c_ref[pl.ds(pl.multiple_of(g * 2 * B, 2 * B), 2 * B), :]

            def half(h, inner):
                rows = pl.ds(pl.multiple_of(h * 512, 512), 512)
                prod[rows, :] = dot_t(r_ref[rows, :], right)
                return inner

            lax.fori_loop(0, 2, half, 0)
            for m in range(2):

                @pl.when(2 * g + m < count)
                def _(m=m):
                    slot = col_ref[a, 2 * g + m]
                    for b in range(8):
                        at = pl.ds(row_ref[a, b] * (8 * B) + slot, B, stride=8)
                        out_ref[at, :] = out_ref[at, :] - prod[b * B : (b + 1) * B, m * B : (m + 1) * B]

            return carry

        lax.fori_loop(0, (count + 1) // 2, pair, 0)


def extend(counts, col_slots, row_slots, front, r0, r1, c0, c1):
    smem = pl.BlockSpec(memory_space=pltpu.SMEM)
    vmem = pl.BlockSpec(memory_space=pltpu.VMEM)
    return pl.pallas_call(
        extend_kernel,
        out_shape=jax.ShapeDtypeStruct(front.shape, F32),
        in_specs=[smem] * 3 + [vmem] * 5,
        out_specs=vmem,
        scratch_shapes=[pltpu.VMEM((8 * B, 2 * B), F32)],
        compiler_params=pltpu.CompilerParams(vmem_limit_bytes=VMEM_BYTES),
        name="extend_add",
    )(counts, col_slots, row_slots, front, r0, r1, c0, c1)


def move(x, target):
    def flat(c):
        return int(np.ravel_multi_index(c, SIZES))

    pairs = [(flat(c), flat(target(*c))) for c in np.ndindex(*SIZES)]
    return lax.ppermute(x, AXES, pairs)


def step_z(by):
    return lambda yhi, x, ylo, z, core: (yhi, x, ylo, (z + by) % 4, core)


def step_x(by):
    return lambda yhi, x, ylo, z, core: (yhi, (x + by) % 4, ylo, z, core)


def step_y(by):
    def target(yhi, x, ylo, z, core):
        y = (yhi * 2 + ylo + by) % 4
        return (y // 2, x, y % 2, z, core)

    return target


def step_first(by):
    return lambda *c: (step_x(by) if c[4] == 0 else step_y(by))(*c)


def step_second(by):
    return lambda *c: (step_y(by) if c[4] == 0 else step_x(by))(*c)


def ring(x, step):
    return x, move(x, step(1)), move(x, step(2)), move(x, step(-1))


def after(x, done):
    return lax.optimization_barrier((x, done))


def axis_groups(stage):
    groups = {}
    for c in np.ndindex(*SIZES):
        yhi, x, ylo, z, core = c
        along_x = core == stage
        key = (core, z, yhi, ylo) if along_x else (core, z, x)
        groups.setdefault(key, []).append((x if along_x else yhi * 2 + ylo, int(np.ravel_multi_index(c, SIZES))))
    return [[device for _, device in sorted(group)] for group in groups.values()]


def swap(x):
    return move(x, lambda yhi, x, ylo, z, core: (yhi, x, ylo, z, 1 - core))


def to_col_group(yhi, x, ylo, z, core):
    shift = z if core == 0 else (z + 2) % 4
    y = (yhi * 2 + ylo + shift) % 4
    return (y // 2, x if core == 0 else 3 - x, y % 2, yhi * 2 + x // 2, ylo)


def pick(x, index):
    return lax.dynamic_index_in_dim(x, index, 0, keepdims=False)


def per_device(child_pivot, child_panel, child_map, panel_mask, parent_front):
    yhi, x, ylo, z, core = (lax.axis_index(name) for name in AXES)
    row = yhi * 4 + x
    y = yhi * 2 + ylo
    at = jnp.stack([yhi, x, ylo, z, core]).astype(jnp.int32)
    n = child_pivot.shape[2]
    np_ = n // PW

    other = swap(pick(child_pivot, 1 - core))
    own = pick(child_pivot, core)
    strip = jnp.where(core == 0, jnp.concatenate([own, other]), jnp.concatenate([other, own]))
    strip = strip.reshape(STRIP, np_, PW).transpose(1, 0, 2)

    def plane(part):
        part = jnp.stack(ring(part, step_z), axis=1)
        return jnp.stack(ring(part, step_first), axis=1).reshape(2, 16 * STRIP, PW)

    mask = pick(pick(panel_mask, ylo), row * 8 + z * 2 + core)
    kept = (child_panel.reshape(B, n // B, B) * mask.astype(BF16)[None, :, None]).reshape(B, n)
    first = plane(strip[:2])
    first, kept = after(first, kept)
    for_col = move(kept, to_col_group)
    back, ahead = move(first, step_second(1)), move(first, step_second(-1))
    far = move(back[:1], step_second(1)), move(ahead[1:], step_second(-1))
    rest = plane(after(strip[2:], first)[0])

    maps = child_map.reshape(2, 8, 8)
    maps = jnp.stack([pick(maps, core), pick(maps, 1 - core)])
    slots = maps // 8
    row_slots = lax.dynamic_index_in_dim(slots, row, 1, keepdims=False)
    by_col = lax.dynamic_slice_in_dim(slots, 2 * z, 2, axis=1)
    needed = by_col % 2 == ylo
    place = jnp.cumsum(needed.astype(jnp.int32), axis=2) - 1
    hit = (place[..., None, :] == jnp.arange(8)[:, None]) & needed[..., None, :]
    i = jnp.arange(8)
    from_z, from_core = (i // 2)[None, :], (i % 2)[None, :]
    from_x = 2 * (z % 2) + jnp.arange(2)[:, None]
    x_of = jnp.where(from_core == 0, from_x, 3 - from_x)
    y_of = (2 * (z // 2) + core + from_z + 2 * from_core) % 4 + 0 * x_of
    where = jnp.where(core == 0, y_of * 4 + x_of, x_of * 4 + y_of)
    order = jnp.sum(jnp.where(hit[0], where[:, None, :], 0), axis=2).astype(jnp.int32)
    col_slots = jnp.sum(jnp.where(hit, (by_col // 2)[..., None, :], 0), axis=3).astype(jnp.int32)
    counts = jnp.sum(needed, axis=2).astype(jnp.int32)

    mine_cols = lax.dynamic_index_in_dim(col_slots, core, 1, keepdims=False)
    mine_counts = lax.dynamic_index_in_dim(counts, core, 1, keepdims=False)
    ask_near = (pick(counts[0], 1 - core)[None], pick(order, 1 - core))
    ask_own = (pick(counts[0], core)[None], pick(order, core))
    small = (mine_cols, mine_counts, row_slots, ask_near, ask_own)

    (small, rest, for_col), arrived = after((small, rest, for_col), (back, ahead) + far)
    mine_cols, mine_counts, row_slots, ask_near, ask_own = small
    back, ahead, *far = arrived
    near_rest = move(rest, step_second(1)), move(rest, step_second(-1))
    for_col = lax.all_gather(for_col, AXES, axis=0, axis_index_groups=axis_groups(0))

    panels = factor_panels(0, n, at, [(first, 0), (back, 0), (far[0], 0), (ahead, 0)], [])
    (near_rest, for_col), panels[0] = after((near_rest, for_col), panels[0])
    back2, ahead2 = near_rest
    far2 = move(back2[:1], step_second(1)), move(ahead2[1:], step_second(-1))
    for_col = lax.all_gather(for_col, AXES, axis=0, axis_index_groups=axis_groups(1))
    panels += factor_panels(1, n, at, [(first, 1), (back, 1), (far[1], 0), (ahead, 1)], panels)
    (far2, kept), panels[1] = after((far2, kept), panels[1])
    row_panel = lax.all_gather(kept, ("ylo", "z", "core"), axis=0)
    pieces = [p for i in range(np_ - 2) for p in [(rest, i), (back2, i), (far2[i], 0), (ahead2, i)]]
    panels += factor_panels(2, n, at, pieces, panels)
    col_panel = for_col.reshape(16, B, n)

    both = jnp.concatenate([ask_near[0], ask_own[0]]), jnp.stack([ask_near[1], ask_own[1]])
    col_near, col_own = solve_both(col_panel, *both, panels)
    col_other = swap(col_near)
    row_panel, col_own = after(row_panel, col_own)
    row_order = core * 8 + jnp.arange(8, dtype=jnp.int32)
    row_side = solve(row_panel, jnp.full((1,), 8, jnp.int32), row_order, panels)
    row_other = swap(row_side)

    front = parent_front.reshape(-1, B)
    out = extend(mine_counts, mine_cols, row_slots, front, row_side, row_other, col_own, col_other)
    return out.reshape(parent_front.shape)


def solution(mesh):
    rows, cols = AXES[:2], AXES[2:]
    split_mesh = Mesh(mesh.devices.reshape(SIZES), AXES)
    front = P(None, rows, None, None, cols, None)
    return jax.shard_map(
        per_device,
        mesh=split_mesh,
        in_specs=(P(None, AXES, None), P(rows, cols, None, None), P(), P(), front),
        out_specs=front,
        check_vma=False,
    )
```
